32 devices in a mesh: parts: 2 (over x), node: 2 (over core), local: 8 (over z, y).
Axes of the slice: x: 2, y: 2, z: 4, core: 2. Of those that a mesh axis runs over, the one named last changes fastest.
Arguments:
- tokens: bfloat16 [4096, 3584], P(('parts', 'node', 'local')), parts along dimension 0, may hold values from -6 to 6
- expert_ids: int32 [4096, 4], P(('parts', 'node', 'local')), parts along dimension 0, may hold values from 0 to 7, all different within a row; in each aligned block of 128 rows (0 to 127, 128 to 255, ...) at most 80 rows name the same one
- combine_weights: bfloat16 [4096, 4], P(('parts', 'node', 'local')), parts along dimension 0, may hold values from 0.19921875 to 1
- gate_weight: bfloat16 [16, 3584, 512], P(('node', 'local')), may hold values from -0.09375 to 0.09375
- up_weight: bfloat16 [16, 3584, 512], P(('node', 'local')), may hold values from -0.09375 to 0.09375
- down_weight: bfloat16 [16, 512, 3584], P(('node', 'local')), may hold values from -0.1875 to 0.1875
Outputs:
- moe_out: bfloat16 [4096, 3584], P(('parts', 'node', 'local')), parts along dimension 0
The draws below stay inside these ranges and needn't reach their ends.
There are 2 independent parts, one for each index of `parts`. The reference program is written for one: setup_inputs(seed, part) draws one part's arguments, and reference() takes and returns one part's arrays. A program takes and returns all parts, laid end to end along the dimension named above; an argument that names none is the same for every part. Nothing has to cross between parts.
Inputs may be any that keep to these rules, and one draw needn't show every extreme that they name: `expert_ids`: each row names 4 different experts. Among the 128 rows of one device, no expert is named by more than 80 rows, and this bound is reached.
All inputs are finite; a program needn't handle non-finite values.
Results may differ from the reference program's by a relative error of at most 0.0072.
Values may be sent and summed in bfloat16 or wider, within the bound.
No kernel may reach another device: no remote copies, remote signals or barrier semaphores. Data moves between devices by JAX's collectives and lax.ppermute only.
A program may use at most 128 MiB of HBM per device.

```python
import math
import jax
import jax.numpy as jnp
import numpy as np
from jax import lax

D = 3584
FF = 1024
TOPK = 4
TOK_DEV = 128
HALF = 512
EXPERTS = 8
CAP = 80
TOKENS = 2048
N_NODE = 2
N_LOCAL = 8


def levels(own_key, dims, cuts, least, top_value):
    loudness = 1.0
    for dim, blocks in cuts:
        draws = jax.random.uniform(jax.random.fold_in(jax.random.fold_in(own_key, 6), dim), (blocks,), jnp.float32, least / len(cuts), top_value / len(cuts))
        loudness = loudness * jnp.repeat(jnp.exp(draws), dims[dim] // blocks).reshape((-1,) + (1,) * (len(dims) - 1 - dim))
    return loudness


def routed_block(stream_key, own, number, rows, amount, top, most, lean):
    order = jax.random.permutation(stream_key, amount)
    heavy_load, usual = portions_of(amount, rows * top, most, lean, True), portions_of(amount, rows * top, most, lean, False)
    places = jnp.arange(amount)

    def named(sizes, turn):
        used = int((sizes > 0).sum())
        fixed = max(1, used // 4)
        passed = fixed + (places - fixed + turn * (used - fixed)) % max(1, amount - fixed)
        return jnp.zeros((amount,), jnp.int32).at[order[jnp.where(places < fixed, places, passed)]].set(jnp.asarray(sizes, jnp.int32))

    sizes = jnp.where(number % 4 == 0, named(heavy_load, number // 4), named(usual, number - number // 4 - 1))
    mixed = jax.random.permutation(jax.random.fold_in(own, 3), amount)
    source_of, taker = mixed[0:amount // 2 * 2:2], mixed[1:amount // 2 * 2:2]
    slack = jnp.minimum(sizes[source_of] - 1, most - sizes[taker]) // 2
    slack = jnp.where((source_of == order[0]) | (taker == order[0]) | (sizes[taker] == 0), 0, jnp.maximum(slack, 0))
    passed = jax.random.randint(jax.random.fold_in(own, 4), (amount // 2,), 0, 1 << 20) % (slack + 1)
    sizes = sizes.at[source_of].add(-passed).at[taker].add(passed)
    items = jnp.searchsorted(jnp.cumsum(sizes), jnp.arange(rows * top), side="right").astype(jnp.int32)
    table = items.reshape(top, rows).T
    table = table[jax.random.permutation(jax.random.fold_in(own, 1), rows)]
    turn = jax.random.randint(jax.random.fold_in(own, 2), (rows, 1), 0, top)
    return jnp.take_along_axis(table, (jnp.arange(top)[None, :] + turn) % top, axis=1)


def portions_of(amount, total, bound, skew, full):
    weights = [(1 << 20) // math.isqrt(grade ** skew) + 1 for grade in range(1, amount + 1)]
    largest = bound if full else min(bound, max(-(-total // amount), total * weights[0] // sum(weights)))
    least = 1 if total - largest >= amount - 1 else 0
    holding, spare = [largest] + [least] * (amount - 1), total - largest - least * (amount - 1)
    while spare > 0:
        free = [i for i in range(1, amount) if holding[i] < largest] or [i for i in range(1, amount) if holding[i] < bound]
        pool, left = sum([weights[i] for i in free]), spare
        for i in free:
            addition = min(bound - holding[i], max(1, left * weights[i] // pool), spare)
            holding[i] = holding[i] + addition
            spare = spare - addition
    return np.array(holding)


def centred(rng, shape, deviation, reach, pieces=(), kind=jnp.bfloat16):
    drawn = deviation * jax.random.normal(rng, shape, jnp.float32)
    if pieces:
        drawn = drawn * levels(rng, shape, pieces, -0.22, 0.18)
    return jnp.clip(drawn, -reach, reach).astype(kind)


def setup_inputs(seed: int = 0, part: int = 0) -> dict:
    arg_keys = jax.random.split(jax.random.key(seed), 7)
    own_keys = jax.random.split(jax.random.fold_in(arg_keys[6], part), 7)
    tokens = centred(own_keys[0], (TOKENS, D), 1.0, 6.0, ((0, 16),))
    expert_ids_keys = jax.random.split(jax.random.fold_in(own_keys[1], 1), TOKENS // TOK_DEV)
    expert_ids_turns = jax.random.permutation(jax.random.fold_in(own_keys[1], 3), TOKENS // TOK_DEV)
    expert_ids = jax.vmap(lambda own, number: routed_block(jax.random.fold_in(own_keys[1], 2), own, number, TOK_DEV, EXPERTS, TOPK, CAP, 2))(expert_ids_keys, expert_ids_turns).reshape((TOKENS, TOPK))
    combine_weights = jnp.clip(0.19921875 + 0.80078125 * jax.random.uniform(own_keys[2], (TOKENS, TOPK), jnp.float32) ** levels(own_keys[2], (TOKENS, TOPK), ((0, 16),), -0.2, 0.2), 0.19921875, 1.0).astype(jnp.bfloat16)
    gate_weight = centred(arg_keys[3], (2 * EXPERTS, D, HALF), D ** -0.5, 0.09375, ((0, 16),))
    up_weight = centred(arg_keys[4], (2 * EXPERTS, D, HALF), D ** -0.5, 0.09375, ((0, 16),))
    down_weight = centred(arg_keys[5], (2 * EXPERTS, HALF, D), FF ** -0.5, 0.1875, ((0, 16),))
    return dict(tokens=tokens, expert_ids=expert_ids, combine_weights=combine_weights, gate_weight=gate_weight, up_weight=up_weight, down_weight=down_weight)


def reference(tokens, expert_ids, combine_weights, gate_weight, up_weight, down_weight):
    per_node = N_LOCAL // 2
    expert_total = N_NODE * N_LOCAL // 2
    most_rows = N_NODE * N_LOCAL * CAP
    row_total = tokens.shape[0]
    weights_wide = combine_weights.astype(jnp.float32)

    def expert_step(totals, expert):
        chosen = expert_ids == expert
        picked = jnp.any(chosen, axis=1)
        picked_count = jnp.sum(picked.astype(jnp.int32))
        row_index = jnp.nonzero(picked, size=most_rows, fill_value=0)[0].astype(jnp.int32)
        is_valid = jnp.arange(most_rows, dtype=jnp.int32) < picked_count
        row_weight = jnp.sum(jnp.where(chosen, weights_wide, 0.0), axis=1)[row_index]
        row_weight = jnp.where(is_valid, row_weight, 0.0)
        row_data = tokens[row_index]
        gate_full = jnp.concatenate([gate_weight[2 * expert], gate_weight[2 * expert + 1]], axis=1)
        up_full = jnp.concatenate([up_weight[2 * expert], up_weight[2 * expert + 1]], axis=1)
        gate_value = jnp.dot(row_data, gate_full, preferred_element_type=jnp.float32)
        up_value = jnp.dot(row_data, up_full, preferred_element_type=jnp.float32)
        hidden = (jax.nn.silu(gate_value) * up_value).astype(jnp.bfloat16)
        lower_half = jnp.dot(hidden[:, :HALF], down_weight[2 * expert], preferred_element_type=jnp.float32).astype(jnp.bfloat16)
        upper_half = jnp.dot(hidden[:, HALF:], down_weight[2 * expert + 1], preferred_element_type=jnp.float32).astype(jnp.bfloat16)
        expert_out = (lower_half.astype(jnp.float32) + upper_half.astype(jnp.float32)).astype(jnp.bfloat16)
        contrib = expert_out.astype(jnp.float32) * row_weight[:, None]
        totals = totals.at[expert // per_node, row_index].add(contrib)
        return totals, None

    start = jnp.zeros((N_NODE, row_total, D), jnp.float32)
    totals, _ = lax.scan(expert_step, start, jnp.arange(expert_total, dtype=jnp.int32))
    rounded = lax.optimization_barrier(totals.astype(jnp.bfloat16))
    return jnp.sum(rounded.astype(jnp.float32), axis=0).astype(jnp.bfloat16)
```

```python
import jax
import jax.numpy as jnp
from jax import lax
from jax.sharding import PartitionSpec as P


def expert_weights(expert_ids, combine_weights, expert_total):
    options = jnp.arange(expert_total, dtype=jnp.int32)
    matches = expert_ids[:, :, None] == options[None, None, :]
    spread = jnp.where(matches, combine_weights.astype(jnp.float32)[:, :, None], 0.0)
    return jnp.sum(spread, axis=1).astype(jnp.bfloat16)


def add_rounded(first, second):
    return (first.astype(jnp.float32) + second.astype(jnp.float32)).astype(jnp.bfloat16)


def on_device(tokens, expert_ids, combine_weights, gate_weight, up_weight, down_weight):
    node_count = lax.axis_size("node")
    local_count = lax.axis_size("local")
    planes = local_count // 2
    expert_total = node_count * planes
    token_count = tokens.shape[0]
    gate_local = gate_weight[0]
    up_local = up_weight[0]
    down_local = down_weight[0]
    node = lax.axis_index("node")
    local = lax.axis_index("local")
    plane = local // 2
    half = local % 2
    expert = node * planes + plane
    low_side = plane < planes // 2

    swap_half = [(i, i ^ 1) for i in range(local_count)]
    swap_node = [(0, 1), (1, 0)]

    def up_pairs(low, high):
        return [(2 * p + h, 2 * p + 2 + h) for p in range(low, high) for h in range(2)]

    def down_pairs(low, high):
        return [(b, a) for a, b in up_pairs(low, high)]

    table = expert_weights(expert_ids, combine_weights, expert_total)
    table = lax.all_gather(table, ("node", "local"), axis=0, tiled=False)
    table = lax.dynamic_index_in_dim(table, expert, axis=2, keepdims=False)
    table = table.reshape(node_count, planes, 2, token_count)

    def weights_of(source):
        row = lax.dynamic_index_in_dim(table, source, axis=1, keepdims=False)
        row = jnp.where(node == 0, row, row[::-1])
        row = jnp.where(half == 0, row, row[:, ::-1])
        return row.reshape(2 * 2 * token_count, 1).astype(jnp.float32)

    from_above, from_below = [tokens], [tokens]
    for step in range(1, planes):
        from_above.append(lax.ppermute(from_above[-1], "local", down_pairs(0, planes - step)))
        from_below.append(lax.ppermute(from_below[-1], "local", up_pairs(step - 1, planes - 1)))

    def compute(block, source):
        other = lax.ppermute(block, "local", swap_half)
        rows = [block, other]
        rows = rows + [lax.ppermute(r, "node", swap_node) for r in rows]
        rows = jnp.concatenate(rows, axis=0)
        gate_value = jnp.dot(rows, gate_local, preferred_element_type=jnp.float32)
        up_value = jnp.dot(rows, up_local, preferred_element_type=jnp.float32)
        hidden = (jax.nn.silu(gate_value) * up_value).astype(jnp.bfloat16)
        out = jnp.dot(hidden, down_local, preferred_element_type=jnp.float32)
        return (out * weights_of(source)).astype(jnp.bfloat16)

    def reduce_chip(out):
        parts = [out[i * token_count : (i + 1) * token_count] for i in range(4)]
        here = add_rounded(parts[0], lax.ppermute(parts[2], "node", swap_node))
        there = add_rounded(parts[1], lax.ppermute(parts[3], "node", swap_node))
        return add_rounded(here, lax.ppermute(there, "local", swap_half))

    outs = [compute(tokens, plane)]
    for k in range(1, planes):
        block = jnp.where(low_side, from_above[k], from_below[k])
        source = jnp.where(low_side, plane + k, plane - k)
        for p in range(planes):
            if p < planes // 2 and k > planes - 1 - p:
                s = k - (planes - 1 - p)
                block = jnp.where(plane == p, from_below[s], block)
                source = jnp.where(plane == p, plane - s, source)
            if p >= planes // 2 and k > p:
                s = k - p
                block = jnp.where(plane == p, from_above[s], block)
                source = jnp.where(plane == p, plane + s, source)
        outs.append(compute(block, source))

    sums = [None] * planes
    going_up, going_down = None, None
    for k in range(planes - 1, -1, -1):
        sums[k] = reduce_chip(outs[k])
    for k in range(planes - 1, 0, -1):
        mine_up, mine_down = sums[k], sums[k]
        for p in range(planes):
            if p >= planes // 2 and k + p < planes:
                mine_up = jnp.where(plane == p, sums[k + p], mine_up)
            if p < planes // 2 and k + planes - 1 - p < planes:
                mine_down = jnp.where(plane == p, sums[k + planes - 1 - p], mine_down)
        if going_up is not None:
            mine_up = add_rounded(mine_up, going_up)
            mine_down = add_rounded(mine_down, going_down)
        going_up = lax.ppermute(mine_up, "local", up_pairs(0, planes - k))
        going_down = lax.ppermute(mine_down, "local", down_pairs(k - 1, planes - 1))
    total = sums[0].astype(jnp.float32) + going_up.astype(jnp.float32) + going_down.astype(jnp.float32)
    return total.astype(jnp.bfloat16)


def solution(mesh):
    in_specs = (
        P(("parts", "node", "local"), None),
        P(("parts", "node", "local"), None),
        P(("parts", "node", "local"), None),
        P(("node", "local"), None, None),
        P(("node", "local"), None, None),
        P(("node", "local"), None, None),
    )
    out_specs = P(("parts", "node", "local"), None)
    return jax.shard_map(
        on_device, mesh=mesh, in_specs=in_specs, out_specs=out_specs, check_vma=False
    )
```

```python
import functools

import jax
import jax.numpy as jnp
from jax import lax
from jax.experimental import pallas as pl
from jax.experimental.pallas import tpu as pltpu
from jax.sharding import PartitionSpec as P

TILE = 256
LANES = 128


def slot_tables(routes, first_expert, expert_count, capacity, expert_total):
    options = jnp.arange(expert_total, dtype=jnp.int32)
    matches = routes[:, :, None] == options[None, None, :]
    counts = jnp.sum(matches.astype(jnp.int32), axis=1)
    before = jnp.cumsum(counts, axis=0) - counts
    rank_in = jnp.sum(jnp.where(matches, before[:, None, :], 0), axis=2)
    local_index = routes - first_expert
    inside = (local_index >= 0) & (local_index < expert_count)
    return (local_index * capacity + rank_in, inside)


def dispatch_matrix(slot_index, inside, total_slots):
    positions = jnp.arange(total_slots, dtype=jnp.int32)
    matches = (slot_index[None, :, :] == positions[:, None, None]) & inside[None, :, :]
    return jnp.sum(matches.astype(jnp.float32), axis=2).astype(jnp.bfloat16)


def weight_matrix(slot_index, inside, weights, total_slots):
    positions = jnp.arange(total_slots, dtype=jnp.int32)
    matches = (slot_index[:, :, None] == positions[None, None, :]) & inside[:, :, None]
    spread = jnp.where(matches, weights.astype(jnp.float32)[:, :, None], 0.0)
    return jnp.sum(spread, axis=1).astype(jnp.bfloat16)


def apply_expert(rows, gate_local, up_local, down_local):
    gate_value = jnp.dot(rows, gate_local, preferred_element_type=jnp.float32)
    up_value = jnp.dot(rows, up_local, preferred_element_type=jnp.float32)
    hidden = (jax.nn.silu(gate_value) * up_value).astype(jnp.bfloat16)
    return jnp.dot(hidden, down_local, preferred_element_type=jnp.float32).astype(jnp.bfloat16)


def packed_exchange(tokens, expert_ids, combine_weights, gate_weight, up_weight, down_weight):
    node_count = lax.axis_size("node")
    local_count = lax.axis_size("local")
    per_node = local_count // 2
    expert_total = node_count * per_node
    token_count = tokens.shape[0]
    model_width = tokens.shape[1]
    top_count = expert_ids.shape[1]
    capacity = token_count * top_count * 5 // (4 * expert_total)
    gate_local = gate_weight[0]
    up_local = up_weight[0]
    down_local = down_weight[0]
    rows_all, weights_all = (
        lax.all_gather(tokens, "node", axis=0, tiled=True),
        lax.all_gather(combine_weights, "node", axis=0, tiled=True),
    )
    routes_all = lax.all_gather(expert_ids, "node", axis=0, tiled=True)
    first_expert = lax.axis_index("node") * per_node
    total_slots = per_node * capacity
    routes_blocks = routes_all.reshape(node_count, token_count, top_count)
    slot_index, inside = jax.vmap(
        lambda routes: slot_tables(routes, first_expert, per_node, capacity, expert_total)
    )(routes_blocks)
    placing = jax.vmap(lambda slots, marks: dispatch_matrix(slots, marks, total_slots))(
        slot_index, inside
    )
    row_blocks = rows_all.reshape(node_count, token_count, model_width)
    packed = jnp.einsum(
        "bst,btd->bsd", placing, row_blocks, preferred_element_type=jnp.float32
    ).astype(jnp.bfloat16)
    packed = packed.reshape(node_count, per_node, capacity, model_width).transpose(1, 0, 2, 3)
    outgoing = jnp.broadcast_to(packed[:, None], (per_node, 2, node_count, capacity, model_width))
    outgoing = outgoing.reshape(local_count, node_count * capacity, model_width)
    rows = lax.all_to_all(outgoing, "local", split_axis=0, concat_axis=0, tiled=True)
    in_shape = rows.shape
    flat_rows = rows.reshape(-1, model_width)
    returned = lax.all_to_all(
        apply_expert(flat_rows, gate_local, up_local, down_local).reshape(in_shape),
        "local",
        split_axis=0,
        concat_axis=0,
        tiled=True,
    )
    returned = returned.reshape(per_node, 2, node_count, capacity, model_width).astype(jnp.float32)
    results = (returned[:, 0] + returned[:, 1]).astype(jnp.bfloat16)
    by_block = results.transpose(1, 0, 2, 3).reshape(node_count, total_slots, model_width)
    weight_blocks = weights_all.reshape(node_count, token_count, top_count)
    mixing = jax.vmap(
        lambda slots, marks, weights: weight_matrix(slots, marks, weights, total_slots)
    )(slot_index, inside, weight_blocks)
    contrib = jnp.einsum(
        "bts,bsd->btd", mixing, by_block, preferred_element_type=jnp.float32
    ).astype(jnp.bfloat16)
    contrib = lax.optimization_barrier(contrib)
    summed_out = lax.psum_scatter(
        contrib.astype(jnp.float32).astype(jnp.bfloat16), "node", scatter_dimension=0, tiled=True
    ).astype(jnp.float32)
    return summed_out[0].astype(jnp.bfloat16)


def expert_weights(expert_ids, combine_weights, expert_total):
    options = jnp.arange(expert_total, dtype=jnp.int32)
    matches = expert_ids[:, :, None] == options[None, None, :]
    spread = jnp.where(matches, combine_weights.astype(jnp.float32)[:, :, None], 0.0)
    return jnp.sum(spread, axis=1).astype(jnp.bfloat16)


def add_rounded(first, second):
    return (first.astype(jnp.float32) + second.astype(jnp.float32)).astype(jnp.bfloat16)


def dot32(a, b):
    return jnp.dot(a, b, preferred_element_type=jnp.float32)


def hidden_kernel(batches, pieces, where_ref, *refs):
    rows_refs = refs[:batches]
    gates = refs[batches : batches + len(pieces)]
    ups = refs[batches + len(pieces) : batches + 2 * len(pieces)]
    out_ref = refs[-1]
    step = pl.program_id(0)
    steps_each = pl.num_programs(0) // batches

    def work(rows):
        gate_value, up_value = None, None
        for (offset, length, kind), g, u in zip(pieces, gates, ups):
            if kind < 0:
                columns = slice(offset, offset + length)
            else:
                columns = pl.ds(pl.multiple_of(where_ref[kind] + offset, LANES), length)
            part = rows[:, columns]
            gate_part, up_part = dot32(part, g[...]), dot32(part, u[...])
            gate_value = gate_part if gate_value is None else gate_value + gate_part
            up_value = up_part if up_value is None else up_value + up_part
        out_ref[...] = (gate_value / (1.0 + jnp.exp(-gate_value)) * up_value).astype(jnp.bfloat16)

    for b in range(batches):
        pl.when(step // steps_each == b)(functools.partial(work, rows_refs[b]))


def hidden_call(where, rows, pieces, gates, ups):
    batches = len(rows)
    steps_each = rows[0].shape[0] // TILE
    width = rows[0].shape[1]
    units = gates[0].shape[1]

    def rows_map(b):
        return lambda i, w: (jnp.clip(i - b * steps_each, 0, steps_each - 1), 0)

    total = batches * steps_each * TILE
    depth = sum(g.shape[0] for g in gates)
    once = pl.Buffered(1)
    return pl.pallas_call(
        functools.partial(hidden_kernel, batches, pieces),
        grid_spec=pltpu.PrefetchScalarGridSpec(
            num_scalar_prefetch=1,
            grid=(batches * steps_each,),
            in_specs=[pl.BlockSpec((TILE, width), rows_map(b)) for b in range(batches)]
            + [pl.BlockSpec(g.shape, lambda i, w: (0, 0), pipeline_mode=once) for g in gates]
            + [pl.BlockSpec(u.shape, lambda i, w: (0, 0), pipeline_mode=once) for u in ups],
            out_specs=pl.BlockSpec((TILE, units), lambda i, w: (i, 0)),
        ),
        out_shape=jax.ShapeDtypeStruct((total, units), jnp.bfloat16),
        compiler_params=pltpu.CompilerParams(vmem_limit_bytes=30 * 2**20),
        cost_estimate=pl.CostEstimate(
            flops=4 * total * depth * units,
            bytes_accessed=2 * (total * width + 2 * depth * units + total * units),
            transcendentals=total * units,
        ),
    )(where, *rows, *gates, *ups)


def down_kernel(batches, first, width, where_ref, *refs):
    spread_refs = refs[:batches]
    own_refs = refs[batches : 2 * batches]
    other_ref, down_ref, near_ref, far_ref, home_ref, away_ref = refs[2 * batches :]
    step = pl.program_id(0)
    steps_each = pl.num_programs(0) // batches
    half = width // 2

    def work(spread, own, out_ref):
        chosen = lax.broadcasted_iota(jnp.int32, spread.shape, 1) == where_ref[2]
        scale = jnp.sum(jnp.where(chosen, spread[...].astype(jnp.float32), 0.0), axis=1, keepdims=True)
        for piece, slot in ((near_ref, where_ref[3]), (far_ref, 1 - where_ref[3])):
            source = pl.ds(pl.multiple_of(first + slot * half, LANES), half)
            target = pl.ds(pl.multiple_of(slot * half, LANES), half)
            value = dot32(own[...], down_ref[:, source]) + dot32(other_ref[...], piece[...])
            out_ref[:, target] = (value * scale).astype(jnp.bfloat16)

    for i in range(batches * steps_each if False else 4):
        b = i * batches // 4
        pl.when(step == i)(
            functools.partial(work, spread_refs[b], own_refs[b], home_ref if i == 0 else away_ref)
        )


def down_call(where, rows, own, other, down_local, near, far, first):
    batches = len(rows)
    steps_each = rows[0].shape[0] // TILE
    units = down_local.shape[0]
    width = 2 * near.shape[1]
    last = rows[0].shape[1] // LANES - 1

    def tile_map(b, column):
        return lambda i, w: (jnp.clip(i - b * steps_each, 0, steps_each - 1), column)

    once = pl.Buffered(1)
    total = batches * steps_each * TILE
    return pl.pallas_call(
        functools.partial(down_kernel, batches, first, width),
        grid_spec=pltpu.PrefetchScalarGridSpec(
            num_scalar_prefetch=1,
            grid=(batches * steps_each,),
            in_specs=[pl.BlockSpec((TILE, LANES), tile_map(b, last)) for b in range(batches)]
            + [pl.BlockSpec((TILE, units), tile_map(b, 0)) for b in range(batches)]
            + [pl.BlockSpec((TILE, units), lambda i, w: (i, 0))]
            + [
                pl.BlockSpec(a.shape, lambda i, w: (0, 0), pipeline_mode=once)
                for a in (down_local, near, far)
            ],
            out_specs=[
                pl.BlockSpec((TILE, width), lambda i, w: (0, 0)),
                pl.BlockSpec((TILE, width), lambda i, w: (jnp.maximum(i - 1, 0), 0)),
            ],
        ),
        out_shape=[
            jax.ShapeDtypeStruct((TILE, width), jnp.bfloat16),
            jax.ShapeDtypeStruct((total - TILE, width), jnp.bfloat16),
        ],
        compiler_params=pltpu.CompilerParams(vmem_limit_bytes=30 * 2**20),
        cost_estimate=pl.CostEstimate(
            flops=4 * total * units * width,
            bytes_accessed=2 * (2 * total * units + 2 * units * width + total * width),
            transcendentals=0,
        ),
    )(where, *rows, *own, other, down_local, near, far)


def line_exchange(tokens, expert_ids, combine_weights, gate_weight, up_weight, down_weight):
    node_count = lax.axis_size("node")
    local_count = lax.axis_size("local")
    planes = local_count // 2
    token_count, model_width = tokens.shape
    expert_total = node_count * planes
    gate_local, up_local, down_local = gate_weight[0], up_weight[0], down_weight[0]
    part = lax.axis_index("parts")
    node = lax.axis_index("node")
    plane = lax.axis_index("local") // 2
    side = plane // 2
    match = side == node
    end = (plane == 0) | (plane == planes - 1)
    both = ("node", "local")
    swap_half = [(i, i ^ 1) for i in range(local_count)]
    swap_two = [(0, 1), (1, 0)]

    def line_pairs(step):
        pairs = []
        for h in range(2):
            pairs += [(2 * (p + 1) + h, 2 * p + h) for p in range(planes - step)]
            pairs += [
                (local_count + 2 * (p - 1) + h, local_count + 2 * p + h) for p in range(step, planes)
            ]
        return pairs

    def back_pairs(step):
        return [(b, a) for a, b in line_pairs(step)]

    def across(x):
        return lax.ppermute(x, "node", swap_two)

    half_depth = model_width // 2
    where = jnp.stack([part * half_depth, (1 - part) * half_depth, node * planes + plane, part])
    where = where.astype(jnp.int32)

    pieces, own_pieces = [], [(0, model_width, -1)]
    sizes = GATE_ROWS, UP_ROWS
    near, far = ([], []), ([], [])

    def fetch(piece):
        first = lax.ppermute(piece, "local", swap_half)
        return first, lax.ppermute(first, "parts", swap_two)

    for m, (array, rows_of) in enumerate(zip((gate_local, up_local), sizes)):
        offset = 0
        for length in rows_of:
            a, b = fetch(lax.dynamic_slice_in_dim(array, part * half_depth + offset, length, 0))
            near[m].append(a)
            far[m].append(b)
            offset += length
    down_near, down_far, firsts = [], [], []
    first = 0
    for width in DOWN_COLUMNS:
        half = width // 2
        a, b = fetch(lax.dynamic_slice_in_dim(down_local, first + part * half, half, 1))
        down_near.append(a)
        down_far.append(b)
        firsts.append(first)
        first += width

    table = expert_weights(expert_ids, combine_weights, expert_total)
    table = jnp.pad(table, ((0, 0), (0, LANES - expert_total)))
    mine = jnp.concatenate([tokens, table], axis=1)
    theirs = across(mine)
    pair = jnp.concatenate(
        [jnp.where(node == 0, mine, theirs), jnp.where(node == 0, theirs, mine)], axis=0
    )
    got, other = [pair], [None]
    for step in range(1, planes):
        got.append(lax.ppermute(got[-1], both, line_pairs(step)))
        other.append(across(got[-1]))
    slot1 = jnp.where(match, got[1], other[1])
    slot2 = jnp.where(match, got[2], other[2])
    slot3 = jnp.where(
        end, jnp.where(match, got[3], other[3]), jnp.where(match, other[1], got[1])
    )
    early = jnp.concatenate([pair, slot1], axis=0)
    late = jnp.concatenate([slot2, slot3], axis=0)

    own_early = hidden_call(where, [early], own_pieces, [gate_local], [up_local])
    own_late = hidden_call(where, [late], own_pieces, [gate_local], [up_local])
    gates = cut_alike(near[0], far[0], sizes[0])
    ups = cut_alike(near[1], far[1], sizes[0])
    offset = 0
    pieces = [(0, half_depth, 0), (0, half_depth, 1)]
    crossed = hidden_call(where, [early, late], pieces, gates, ups)

    results = []
    for k in range(len(DOWN_COLUMNS)):
        home, away = down_call(
            where, [early, late], [own_early, own_late], crossed,
            down_local, down_near[k], down_far[k], firsts[k],
        )
        away = add_rounded(away, across(away))
        s1, s2, s3 = (away[i * TILE : (i + 1) * TILE] for i in range(3))
        moving = lax.ppermute(s3, both, back_pairs(3))
        moving = lax.ppermute(add_rounded(s2, moving), both, back_pairs(2))
        moving = lax.ppermute(add_rounded(jnp.where(match, s1, s3), moving), both, back_pairs(1))
        kept = moving.astype(jnp.float32) + home.astype(jnp.float32)
        low, high = kept[:token_count], kept[token_count:]
        sent = jnp.where(node == 0, high, low).astype(jnp.bfloat16)
        results.append((jnp.where(node == 0, low, high) + across(sent).astype(jnp.float32)).astype(jnp.bfloat16))
    return jnp.concatenate(results, axis=1)


GATE_ROWS = (256, 512, 1024)
UP_ROWS = (1024, 512, 256)
DOWN_COLUMNS = (1024, 1280, 1280)


def cut_alike(near, far, sizes):
    return [jnp.concatenate(near, axis=0), jnp.concatenate(far, axis=0)]


def on_device(tokens, expert_ids, combine_weights, gate_weight, up_weight, down_weight):
    line = (
        lax.axis_size("parts") == 2
        and lax.axis_size("node") == 2
        and lax.axis_size("local") == 8
        and tokens.shape == (128, 3584)
        and gate_weight.shape[2] == 512
    )
    form = line_exchange if line else packed_exchange
    return form(tokens, expert_ids, combine_weights, gate_weight, up_weight, down_weight)


def solution(mesh):
    in_specs = (
        P(("parts", "node", "local"), None),
        P(("parts", "node", "local"), None),
        P(("parts", "node", "local"), None),
        P(("node", "local"), None, None),
        P(("node", "local"), None, None),
        P(("node", "local"), None, None),
    )
    out_specs = P(("parts", "node", "local"), None)
    return jax.shard_map(
        on_device, mesh=mesh, in_specs=in_specs, out_specs=out_specs, check_vma=False
    )
```

```python
import functools

import jax
import jax.numpy as jnp
from jax import lax
from jax.experimental import pallas as pl
from jax.experimental.pallas import tpu as pltpu
from jax.sharding import PartitionSpec as P

TILE = 256
LANES = 128
STEPS = 4
GATE_ROWS = (512, 768, 512)
UP_ROWS = (512, 896, 384)
DOWN_COLUMNS = (768, 1536, 1280)


def slot_tables(routes, first_expert, expert_count, capacity, expert_total):
    options = jnp.arange(expert_total, dtype=jnp.int32)
    matches = routes[:, :, None] == options[None, None, :]
    counts = jnp.sum(matches.astype(jnp.int32), axis=1)
    before = jnp.cumsum(counts, axis=0) - counts
    rank_in = jnp.sum(jnp.where(matches, before[:, None, :], 0), axis=2)
    local_index = routes - first_expert
    inside = (local_index >= 0) & (local_index < expert_count)
    return (local_index * capacity + rank_in, inside)


def dispatch_matrix(slot_index, inside, total_slots):
    positions = jnp.arange(total_slots, dtype=jnp.int32)
    matches = (slot_index[None, :, :] == positions[:, None, None]) & inside[None, :, :]
    return jnp.sum(matches.astype(jnp.float32), axis=2).astype(jnp.bfloat16)


def weight_matrix(slot_index, inside, weights, total_slots):
    positions = jnp.arange(total_slots, dtype=jnp.int32)
    matches = (slot_index[:, :, None] == positions[None, None, :]) & inside[:, :, None]
    spread = jnp.where(matches, weights.astype(jnp.float32)[:, :, None], 0.0)
    return jnp.sum(spread, axis=1).astype(jnp.bfloat16)


def apply_expert(rows, gate_local, up_local, down_local):
    gate_value = jnp.dot(rows, gate_local, preferred_element_type=jnp.float32)
    up_value = jnp.dot(rows, up_local, preferred_element_type=jnp.float32)
    hidden = (jax.nn.silu(gate_value) * up_value).astype(jnp.bfloat16)
    return jnp.dot(hidden, down_local, preferred_element_type=jnp.float32).astype(jnp.bfloat16)


def packed_exchange(tokens, expert_ids, combine_weights, gate_weight, up_weight, down_weight):
    node_count = lax.axis_size("node")
    local_count = lax.axis_size("local")
    per_node = local_count // 2
    expert_total = node_count * per_node
    token_count = tokens.shape[0]
    model_width = tokens.shape[1]
    top_count = expert_ids.shape[1]
    capacity = token_count * top_count * 5 // (4 * expert_total)
    gate_local = gate_weight[0]
    up_local = up_weight[0]
    down_local = down_weight[0]
    rows_all, weights_all = (
        lax.all_gather(tokens, "node", axis=0, tiled=True),
        lax.all_gather(combine_weights, "node", axis=0, tiled=True),
    )
    routes_all = lax.all_gather(expert_ids, "node", axis=0, tiled=True)
    first_expert = lax.axis_index("node") * per_node
    total_slots = per_node * capacity
    routes_blocks = routes_all.reshape(node_count, token_count, top_count)
    slot_index, inside = jax.vmap(
        lambda routes: slot_tables(routes, first_expert, per_node, capacity, expert_total)
    )(routes_blocks)
    placing = jax.vmap(lambda slots, marks: dispatch_matrix(slots, marks, total_slots))(
        slot_index, inside
    )
    row_blocks = rows_all.reshape(node_count, token_count, model_width)
    packed = jnp.einsum(
        "bst,btd->bsd", placing, row_blocks, preferred_element_type=jnp.float32
    ).astype(jnp.bfloat16)
    packed = packed.reshape(node_count, per_node, capacity, model_width).transpose(1, 0, 2, 3)
    outgoing = jnp.broadcast_to(packed[:, None], (per_node, 2, node_count, capacity, model_width))
    outgoing = outgoing.reshape(local_count, node_count * capacity, model_width)
    rows = lax.all_to_all(outgoing, "local", split_axis=0, concat_axis=0, tiled=True)
    in_shape = rows.shape
    flat_rows = rows.reshape(-1, model_width)
    returned = lax.all_to_all(
        apply_expert(flat_rows, gate_local, up_local, down_local).reshape(in_shape),
        "local",
        split_axis=0,
        concat_axis=0,
        tiled=True,
    )
    returned = returned.reshape(per_node, 2, node_count, capacity, model_width).astype(jnp.float32)
    results = (returned[:, 0] + returned[:, 1]).astype(jnp.bfloat16)
    by_block = results.transpose(1, 0, 2, 3).reshape(node_count, total_slots, model_width)
    weight_blocks = weights_all.reshape(node_count, token_count, top_count)
    mixing = jax.vmap(
        lambda slots, marks, weights: weight_matrix(slots, marks, weights, total_slots)
    )(slot_index, inside, weight_blocks)
    contrib = jnp.einsum(
        "bts,bsd->btd", mixing, by_block, preferred_element_type=jnp.float32
    ).astype(jnp.bfloat16)
    contrib = lax.optimization_barrier(contrib)
    summed_out = lax.psum_scatter(
        contrib.astype(jnp.float32).astype(jnp.bfloat16), "node", scatter_dimension=0, tiled=True
    ).astype(jnp.float32)
    return summed_out[0].astype(jnp.bfloat16)


def expert_weights(expert_ids, combine_weights, expert_total):
    options = jnp.arange(expert_total, dtype=jnp.int32)
    matches = expert_ids[:, :, None] == options[None, None, :]
    spread = jnp.where(matches, combine_weights.astype(jnp.float32)[:, :, None], 0.0)
    return jnp.sum(spread, axis=1).astype(jnp.bfloat16)


def add_rounded(first, second):
    return (first.astype(jnp.float32) + second.astype(jnp.float32)).astype(jnp.bfloat16)


def after(x, *earlier):
    return lax.optimization_barrier((x, *earlier))[0] if earlier else x


def dot32(a, b):
    return jnp.dot(a, b, preferred_element_type=jnp.float32)


def hidden_kernel(batches, gate_pieces, up_pieces, where_ref, *refs):
    rows_refs = refs[:batches]
    gates = refs[batches : batches + len(gate_pieces)]
    ups = refs[batches + len(gate_pieces) : -1]
    out_ref = refs[-1]
    step = pl.program_id(0)
    steps_each = pl.num_programs(0) // batches

    def product(rows, pieces, weights):
        total = None
        for (offset, kind), w in zip(pieces, weights):
            if kind < 0:
                columns = slice(offset, offset + w.shape[0])
            else:
                columns = pl.ds(pl.multiple_of(where_ref[kind] + offset, LANES), w.shape[0])
            value = dot32(rows[:, columns], w[...])
            total = value if total is None else total + value
        return total

    def work(rows):
        gate_value = product(rows, gate_pieces, gates)
        up_value = product(rows, up_pieces, ups)
        out_ref[...] = (gate_value / (1.0 + jnp.exp(-gate_value)) * up_value).astype(jnp.bfloat16)

    for b in range(batches):
        pl.when(step // steps_each == b)(functools.partial(work, rows_refs[b]))


def hidden_call(where, rows, gate_parts, up_parts):
    gate_pieces, up_pieces = [p[:2] for p in gate_parts], [p[:2] for p in up_parts]
    gates, ups = [p[2] for p in gate_parts], [p[2] for p in up_parts]
    blocks = [(p[3], p[4]) if len(p) > 3 else (0, p[2].shape[0]) for p in gate_parts + up_parts]
    batches = len(rows)
    steps_each = rows[0].shape[0] // TILE
    width = rows[0].shape[1]
    units = gates[0].shape[1]

    def rows_map(b):
        return lambda i, w: (jnp.clip(i - b * steps_each, 0, steps_each - 1), 0)

    total = batches * steps_each * TILE
    depth = width - LANES
    once = pl.Buffered(1)

    def block_map(block):
        return lambda i, w: (block, 0)

    return pl.pallas_call(
        functools.partial(hidden_kernel, batches, gate_pieces, up_pieces),
        grid_spec=pltpu.PrefetchScalarGridSpec(
            num_scalar_prefetch=1,
            grid=(batches * steps_each,),
            in_specs=[pl.BlockSpec((TILE, width), rows_map(b)) for b in range(batches)]
            + [
                pl.BlockSpec((length, units), block_map(block), pipeline_mode=once)
                for block, length in blocks
            ],
            out_specs=pl.BlockSpec((TILE, units), lambda i, w: (i, 0)),
        ),
        out_shape=jax.ShapeDtypeStruct((total, units), jnp.bfloat16),
        compiler_params=pltpu.CompilerParams(vmem_limit_bytes=30 * 2**20),
        cost_estimate=pl.CostEstimate(
            flops=4 * total * depth * units,
            bytes_accessed=2 * (total * width + 2 * depth * units + total * units),
            transcendentals=total * units,
        ),
    )(where, *rows, *gates, *ups)


def down_kernel(batches, first, width, where_ref, *refs):
    spread_refs = refs[:batches]
    own_refs = refs[batches : 2 * batches]
    other_ref, down_ref, near_ref, far_ref, home_ref, away_ref = refs[2 * batches :]
    step = pl.program_id(0)
    half = width // 2

    def work(spread, own, out_ref):
        chosen = lax.broadcasted_iota(jnp.int32, spread.shape, 1) == where_ref[2]
        scale = jnp.sum(jnp.where(chosen, spread[...].astype(jnp.float32), 0.0), axis=1, keepdims=True)
        for piece, slot in ((near_ref, where_ref[3]), (far_ref, 1 - where_ref[3])):
            source = pl.ds(pl.multiple_of(first + slot * half, LANES), half)
            target = pl.ds(pl.multiple_of(slot * half, LANES), half)
            value = dot32(own[...], down_ref[:, source]) + dot32(other_ref[...], piece[...])
            out_ref[:, target] = (value * scale).astype(jnp.bfloat16)

    for i in range(STEPS):
        b = i * batches // STEPS
        pl.when(step == i)(
            functools.partial(work, spread_refs[b], own_refs[b], home_ref if i == 0 else away_ref)
        )


def down_call(where, rows, own, other, down_local, near, far, first):
    batches = len(rows)
    steps_each = rows[0].shape[0] // TILE
    units = down_local.shape[0]
    width = 2 * near.shape[1]
    last = rows[0].shape[1] // LANES - 1

    def tile_map(b, column):
        return lambda i, w: (jnp.clip(i - b * steps_each, 0, steps_each - 1), column)

    once = pl.Buffered(1)
    total = batches * steps_each * TILE
    return pl.pallas_call(
        functools.partial(down_kernel, batches, first, width),
        grid_spec=pltpu.PrefetchScalarGridSpec(
            num_scalar_prefetch=1,
            grid=(batches * steps_each,),
            in_specs=[pl.BlockSpec((TILE, LANES), tile_map(b, last)) for b in range(batches)]
            + [pl.BlockSpec((TILE, units), tile_map(b, 0)) for b in range(batches)]
            + [pl.BlockSpec((TILE, units), lambda i, w: (i, 0))]
            + [
                pl.BlockSpec(a.shape, lambda i, w: (0, 0), pipeline_mode=once)
                for a in (down_local, near, far)
            ],
            out_specs=[
                pl.BlockSpec((TILE, width), lambda i, w: (0, 0)),
                pl.BlockSpec((TILE, width), lambda i, w: (jnp.maximum(i - 1, 0), 0)),
            ],
        ),
        out_shape=[
            jax.ShapeDtypeStruct((TILE, width), jnp.bfloat16),
            jax.ShapeDtypeStruct((total - TILE, width), jnp.bfloat16),
        ],
        compiler_params=pltpu.CompilerParams(vmem_limit_bytes=30 * 2**20),
        cost_estimate=pl.CostEstimate(
            flops=4 * total * units * width,
            bytes_accessed=2 * (2 * total * units + 2 * units * width + total * width),
            transcendentals=0,
        ),
    )(where, *rows, *own, other, down_local, near, far)


def line_exchange(tokens, expert_ids, combine_weights, gate_weight, up_weight, down_weight):
    node_count = lax.axis_size("node")
    local_count = lax.axis_size("local")
    planes = local_count // 2
    token_count, model_width = tokens.shape
    expert_total = node_count * planes
    gate_local, up_local, down_local = gate_weight[0], up_weight[0], down_weight[0]
    part = lax.axis_index("parts")
    node = lax.axis_index("node")
    plane = lax.axis_index("local") // 2
    side = plane // 2
    match = side == node
    end = (plane == 0) | (plane == planes - 1)
    both = ("node", "local")
    swap_half = [(i, i ^ 1) for i in range(local_count)]
    swap_two = [(0, 1), (1, 0)]

    def line_pairs(step):
        pairs = []
        for h in range(2):
            pairs += [(2 * (p + 1) + h, 2 * p + h) for p in range(planes - step)]
            pairs += [
                (local_count + 2 * (p - 1) + h, local_count + 2 * p + h) for p in range(step, planes)
            ]
        return pairs

    def back_pairs(step):
        return [(b, a) for a, b in line_pairs(step)]

    def across(x):
        return lax.ppermute(x, "node", swap_two)

    half_depth = model_width // 2
    where = jnp.stack([part * half_depth, (1 - part) * half_depth, node * planes + plane, part])
    where = where.astype(jnp.int32)

    def cut(array, offset, length, dim=0):
        begin = part * (half_depth if dim == 0 else length) + offset
        return lax.dynamic_slice_in_dim(array, begin, length, dim)

    def swap(x):
        return lax.ppermute(x, "local", swap_half)

    def relay(x):
        return lax.ppermute(x, "parts", swap_two)

    def line(x, step):
        return lax.ppermute(x, both, line_pairs(step))

    together = lax.optimization_barrier
    g0, g1, g2 = GATE_ROWS
    u0, u1, u2 = UP_ROWS
    d0, d1, d2 = (w // 2 for w in DOWN_COLUMNS)

    table = expert_weights(expert_ids, combine_weights, expert_total)
    table = jnp.pad(table, ((0, 0), (0, LANES - expert_total)))
    mine = jnp.concatenate([tokens, table], axis=1)

    gate_a = swap(cut(gate_local, 0, g0))
    theirs = across(mine)
    pair = jnp.concatenate(
        [jnp.where(node == 0, mine, theirs), jnp.where(node == 0, theirs, mine)], axis=0
    )
    pair, piece = together((pair, cut(gate_local, g0, g1)))
    got1, gate_b, gate_ax = line(pair, 1), swap(piece), relay(gate_a)
    piece = jnp.concatenate([cut(gate_local, g0 + g1, g2), cut(up_local, 0, u0)], axis=0)
    got1, gate_b, gate_ax, piece = together((got1, gate_b, gate_ax, piece))
    got2, both_c, gate_bx = line(got1, 2), swap(piece), relay(gate_b)
    other1 = across(got1)
    pieces = cut(up_local, u0, u1), cut(down_local, 0, d0, 1)
    got2, both_c, gate_bx, other1, pieces = together((got2, both_c, gate_bx, other1, pieces))
    got3, up_b, both_cx, down_a = line(got2, 3), swap(pieces[0]), relay(both_c), swap(pieces[1])
    other2 = across(got2)
    slot1 = jnp.where(match, got1, other1)
    early = jnp.concatenate([pair, slot1], axis=0)
    own = [(0, -1, gate_local)], [(0, -1, up_local)]
    own_early = hidden_call(where, [early], *own)
    rest = u0 + u1
    piece = jnp.concatenate([up_local[rest:half_depth], up_local[half_depth + rest :]], axis=0)
    got3, up_b, both_cx, other2, own_early, piece = together(
        (got3, up_b, both_cx, other2, own_early, piece)
    )
    up_bx, up_c = relay(up_b), swap(piece)
    other3 = across(got3)
    slot2 = jnp.where(match, got2, other2)
    slot3 = jnp.where(
        end,
        jnp.where(match, got3, other3),
        jnp.where(match, after(other1, got3), after(got1, got3)),
    )
    late = jnp.concatenate([slot2, slot3], axis=0)
    own_late = hidden_call(where, [late], *own)
    pieces = cut(down_local, 2 * d0, d1, 1), cut(down_local, 2 * (d0 + d1), d2, 1)
    up_bx, up_c, down_a, own_late, pieces = together((up_bx, up_c, down_a, own_late, pieces))
    down_ax, down_b = relay(down_a), swap(pieces[0])
    crossed = hidden_call(
        where, [early, late],
        [
            (0, 0, gate_a), (g0, 0, gate_b), (g0 + g1, 0, both_c, 0, g2),
            (0, 1, gate_ax), (g0, 1, gate_bx), (g0 + g1, 1, both_cx, 0, g2),
        ],
        [
            (0, 0, both_c, g2 // u0, u0), (u0, 0, up_b),
            (0, 1, both_cx, g2 // u0, u0), (u0, 1, up_bx),
            (rest, -1, up_c, 0, u2), (half_depth + rest, -1, up_c, 1, u2),
        ],
    )
    down_ax, crossed, piece = together((down_ax, crossed, pieces[1]))

    def expert(first, near, far, *earlier):
        return down_call(
            after(where, *earlier), [early, late], [own_early, own_late], crossed,
            down_local, near, far, first,
        )

    def step(rows, moving, k):
        rows = rows if moving is None else add_rounded(rows, moving)
        return lax.ppermute(rows, both, back_pairs(k))

    def thirds(away, arrived):
        away = add_rounded(away, arrived)
        s1, s2, s3 = (away[i * TILE : (i + 1) * TILE] for i in range(3))
        return jnp.where(match, s1, s3), s2, s3

    def finish(home, moving):
        kept = moving.astype(jnp.float32) + home.astype(jnp.float32)
        low, high = kept[:token_count], kept[token_count:]
        sent = across(jnp.where(node == 0, high, low).astype(jnp.bfloat16))
        return (jnp.where(node == 0, low, high) + sent.astype(jnp.float32)).astype(jnp.bfloat16)

    home_a, away_a = expert(0, down_a, down_ax)
    down_bx = relay(down_b)
    down_c = swap(piece)
    a1, a2, a3 = thirds(away_a, across(after(away_a, down_b)))
    moving_a = step(a3, None, 3)
    moving_a = step(after(a2, down_c), moving_a, 2)
    down_bx, down_c, a1 = together((down_bx, down_c, a1))
    down_cx = relay(down_c)
    home_b, away_b = expert(2 * d0, down_b, down_bx, moving_a)
    moving_a = step(a1, moving_a, 1)
    b1, b2, b3 = thirds(away_b, across(away_b))
    moving_b = step(b3, None, 3)
    home_c, away_c = expert(2 * (d0 + d1), down_c, down_cx, b3)
    c1, c2, c3 = thirds(away_c, across(away_c))
    moving_c = step(c3, None, 3)
    moving_b = step(b2, moving_b, 2)
    moving_c = step(c2, moving_c, 2)
    moving_b = step(b1, moving_b, 1)
    moving_c = step(c1, moving_c, 1)
    results = [finish(home_a, moving_a), finish(home_b, moving_b), finish(home_c, moving_c)]
    return jnp.concatenate(results, axis=1)


def on_device(tokens, expert_ids, combine_weights, gate_weight, up_weight, down_weight):
    line = (
        lax.axis_size("parts") == 2
        and lax.axis_size("node") == 2
        and lax.axis_size("local") == 8
        and tokens.shape == (128, 3584)
        and gate_weight.shape[2] == 512
    )
    form = line_exchange if line else packed_exchange
    return form(tokens, expert_ids, combine_weights, gate_weight, up_weight, down_weight)


def solution(mesh):
    in_specs = (
        P(("parts", "node", "local"), None),
        P(("parts", "node", "local"), None),
        P(("parts", "node", "local"), None),
        P(("node", "local"), None, None),
        P(("node", "local"), None, None),
        P(("node", "local"), None, None),
    )
    out_specs = P(("parts", "node", "local"), None)
    return jax.shard_map(
        on_device, mesh=mesh, in_specs=in_specs, out_specs=out_specs, check_vma=False
    )
```

```python
import functools

import jax
import jax.numpy as jnp
from jax import lax
from jax.experimental import pallas as pl
from jax.experimental.pallas import tpu as pltpu
from jax.sharding import PartitionSpec as P

TILE = 256
LANES = 128
STEPS = 4
GATE_ROWS = (512, 768, 512)
UP_ROWS = (512, 896, 384)
DOWN_COLUMNS = (1024, 1536, 1024)


def slot_tables(routes, first_expert, expert_count, capacity, expert_total):
    options = jnp.arange(expert_total, dtype=jnp.int32)
    matches = routes[:, :, None] == options[None, None, :]
    counts = jnp.sum(matches.astype(jnp.int32), axis=1)
    before = jnp.cumsum(counts, axis=0) - counts
    rank_in = jnp.sum(jnp.where(matches, before[:, None, :], 0), axis=2)
    local_index = routes - first_expert
    inside = (local_index >= 0) & (local_index < expert_count)
    return (local_index * capacity + rank_in, inside)


def dispatch_matrix(slot_index, inside, total_slots):
    positions = jnp.arange(total_slots, dtype=jnp.int32)
    matches = (slot_index[None, :, :] == positions[:, None, None]) & inside[None, :, :]
    return jnp.sum(matches.astype(jnp.float32), axis=2).astype(jnp.bfloat16)


def weight_matrix(slot_index, inside, weights, total_slots):
    positions = jnp.arange(total_slots, dtype=jnp.int32)
    matches = (slot_index[:, :, None] == positions[None, None, :]) & inside[:, :, None]
    spread = jnp.where(matches, weights.astype(jnp.float32)[:, :, None], 0.0)
    return jnp.sum(spread, axis=1).astype(jnp.bfloat16)


def apply_expert(rows, gate_local, up_local, down_local):
    gate_value = jnp.dot(rows, gate_local, preferred_element_type=jnp.float32)
    up_value = jnp.dot(rows, up_local, preferred_element_type=jnp.float32)
    hidden = (jax.nn.silu(gate_value) * up_value).astype(jnp.bfloat16)
    return jnp.dot(hidden, down_local, preferred_element_type=jnp.float32).astype(jnp.bfloat16)


def packed_exchange(tokens, expert_ids, combine_weights, gate_weight, up_weight, down_weight):
    node_count = lax.axis_size("node")
    local_count = lax.axis_size("local")
    per_node = local_count // 2
    expert_total = node_count * per_node
    token_count = tokens.shape[0]
    model_width = tokens.shape[1]
    top_count = expert_ids.shape[1]
    capacity = token_count * top_count * 5 // (4 * expert_total)
    gate_local = gate_weight[0]
    up_local = up_weight[0]
    down_local = down_weight[0]
    rows_all, weights_all = (
        lax.all_gather(tokens, "node", axis=0, tiled=True),
        lax.all_gather(combine_weights, "node", axis=0, tiled=True),
    )
    routes_all = lax.all_gather(expert_ids, "node", axis=0, tiled=True)
    first_expert = lax.axis_index("node") * per_node
    total_slots = per_node * capacity
    routes_blocks = routes_all.reshape(node_count, token_count, top_count)
    slot_index, inside = jax.vmap(
        lambda routes: slot_tables(routes, first_expert, per_node, capacity, expert_total)
    )(routes_blocks)
    placing = jax.vmap(lambda slots, marks: dispatch_matrix(slots, marks, total_slots))(
        slot_index, inside
    )
    row_blocks = rows_all.reshape(node_count, token_count, model_width)
    packed = jnp.einsum(
        "bst,btd->bsd", placing, row_blocks, preferred_element_type=jnp.float32
    ).astype(jnp.bfloat16)
    packed = packed.reshape(node_count, per_node, capacity, model_width).transpose(1, 0, 2, 3)
    outgoing = jnp.broadcast_to(packed[:, None], (per_node, 2, node_count, capacity, model_width))
    outgoing = outgoing.reshape(local_count, node_count * capacity, model_width)
    rows = lax.all_to_all(outgoing, "local", split_axis=0, concat_axis=0, tiled=True)
    in_shape = rows.shape
    flat_rows = rows.reshape(-1, model_width)
    returned = lax.all_to_all(
        apply_expert(flat_rows, gate_local, up_local, down_local).reshape(in_shape),
        "local",
        split_axis=0,
        concat_axis=0,
        tiled=True,
    )
    returned = returned.reshape(per_node, 2, node_count, capacity, model_width).astype(jnp.float32)
    results = (returned[:, 0] + returned[:, 1]).astype(jnp.bfloat16)
    by_block = results.transpose(1, 0, 2, 3).reshape(node_count, total_slots, model_width)
    weight_blocks = weights_all.reshape(node_count, token_count, top_count)
    mixing = jax.vmap(
        lambda slots, marks, weights: weight_matrix(slots, marks, weights, total_slots)
    )(slot_index, inside, weight_blocks)
    contrib = jnp.einsum(
        "bts,bsd->btd", mixing, by_block, preferred_element_type=jnp.float32
    ).astype(jnp.bfloat16)
    contrib = lax.optimization_barrier(contrib)
    summed_out = lax.psum_scatter(
        contrib.astype(jnp.float32).astype(jnp.bfloat16), "node", scatter_dimension=0, tiled=True
    ).astype(jnp.float32)
    return summed_out[0].astype(jnp.bfloat16)


def expert_weights(expert_ids, combine_weights, expert_total):
    options = jnp.arange(expert_total, dtype=jnp.int32)
    matches = expert_ids[:, :, None] == options[None, None, :]
    spread = jnp.where(matches, combine_weights.astype(jnp.float32)[:, :, None], 0.0)
    return jnp.sum(spread, axis=1).astype(jnp.bfloat16)


def add_rounded(first, second):
    return (first.astype(jnp.float32) + second.astype(jnp.float32)).astype(jnp.bfloat16)


def after(x, *earlier):
    return lax.optimization_barrier((x, *earlier))[0] if earlier else x


def dot32(a, b):
    return jnp.dot(a, b, preferred_element_type=jnp.float32)


def hidden_kernel(batches, gate_pieces, up_pieces, where_ref, *refs):
    rows_refs = refs[:batches]
    gates = refs[batches : batches + len(gate_pieces)]
    ups = refs[batches + len(gate_pieces) : -1]
    out_ref = refs[-1]
    step = pl.program_id(0)
    steps_each = pl.num_programs(0) // batches

    def product(rows, pieces, weights):
        total = None
        for (offset, kind), w in zip(pieces, weights):
            if kind < 0:
                columns = slice(offset, offset + w.shape[0])
            else:
                columns = pl.ds(pl.multiple_of(where_ref[kind] + offset, LANES), w.shape[0])
            value = dot32(rows[:, columns], w[...])
            total = value if total is None else total + value
        return total

    def work(rows):
        gate_value = product(rows, gate_pieces, gates)
        up_value = product(rows, up_pieces, ups)
        out_ref[...] = (gate_value / (1.0 + jnp.exp(-gate_value)) * up_value).astype(jnp.bfloat16)

    for b in range(batches):
        pl.when(step // steps_each == b)(functools.partial(work, rows_refs[b]))


def hidden_call(where, rows, gate_parts, up_parts):
    gate_pieces, up_pieces = [p[:2] for p in gate_parts], [p[:2] for p in up_parts]
    gates, ups = [p[2] for p in gate_parts], [p[2] for p in up_parts]
    blocks = [(p[3], p[4]) if len(p) > 3 else (0, p[2].shape[0]) for p in gate_parts + up_parts]
    batches = len(rows)
    steps_each = rows[0].shape[0] // TILE
    width = rows[0].shape[1]
    units = gates[0].shape[1]

    def rows_map(b):
        return lambda i, w: (jnp.clip(i - b * steps_each, 0, steps_each - 1), 0)

    total = batches * steps_each * TILE
    depth = width - LANES
    once = pl.Buffered(1)

    def block_map(block):
        return lambda i, w: (block, 0)

    return pl.pallas_call(
        functools.partial(hidden_kernel, batches, gate_pieces, up_pieces),
        grid_spec=pltpu.PrefetchScalarGridSpec(
            num_scalar_prefetch=1,
            grid=(batches * steps_each,),
            in_specs=[pl.BlockSpec((TILE, width), rows_map(b)) for b in range(batches)]
            + [
                pl.BlockSpec((length, units), block_map(block), pipeline_mode=once)
                for block, length in blocks
            ],
            out_specs=pl.BlockSpec((TILE, units), lambda i, w: (i, 0)),
        ),
        out_shape=jax.ShapeDtypeStruct((total, units), jnp.bfloat16),
        compiler_params=pltpu.CompilerParams(vmem_limit_bytes=30 * 2**20),
        cost_estimate=pl.CostEstimate(
            flops=4 * total * depth * units,
            bytes_accessed=2 * (total * width + 2 * depth * units + total * units),
            transcendentals=total * units,
        ),
    )(where, *rows, *gates, *ups)


def down_kernel(batches, first, width, where_ref, *refs):
    spread_refs = refs[:batches]
    own_refs = refs[batches : 2 * batches]
    other_ref, down_ref, near_ref, far_ref, home_ref, away_ref = refs[2 * batches :]
    step = pl.program_id(0)
    half = width // 2

    def work(spread, own, out_ref):
        chosen = lax.broadcasted_iota(jnp.int32, spread.shape, 1) == where_ref[2]
        scale = jnp.sum(jnp.where(chosen, spread[...].astype(jnp.float32), 0.0), axis=1, keepdims=True)
        for piece, slot in ((near_ref, where_ref[3]), (far_ref, 1 - where_ref[3])):
            source = pl.ds(pl.multiple_of(first + slot * half, LANES), half)
            target = pl.ds(pl.multiple_of(slot * half, LANES), half)
            value = dot32(own[...], down_ref[:, source]) + dot32(other_ref[...], piece[...])
            out_ref[:, target] = (value * scale).astype(jnp.bfloat16)

    for i in range(STEPS):
        b = i * batches // STEPS
        pl.when(step == i)(
            functools.partial(work, spread_refs[b], own_refs[b], home_ref if i == 0 else away_ref)
        )


def down_call(where, rows, own, other, down_local, near, far, first):
    batches = len(rows)
    steps_each = rows[0].shape[0] // TILE
    units = down_local.shape[0]
    width = 2 * near.shape[1]
    last = rows[0].shape[1] // LANES - 1

    def tile_map(b, column):
        return lambda i, w: (jnp.clip(i - b * steps_each, 0, steps_each - 1), column)

    once = pl.Buffered(1)
    total = batches * steps_each * TILE
    return pl.pallas_call(
        functools.partial(down_kernel, batches, first, width),
        grid_spec=pltpu.PrefetchScalarGridSpec(
            num_scalar_prefetch=1,
            grid=(batches * steps_each,),
            in_specs=[pl.BlockSpec((TILE, LANES), tile_map(b, last)) for b in range(batches)]
            + [pl.BlockSpec((TILE, units), tile_map(b, 0)) for b in range(batches)]
            + [pl.BlockSpec((TILE, units), lambda i, w: (i, 0))]
            + [
                pl.BlockSpec(a.shape, lambda i, w: (0, 0), pipeline_mode=once)
                for a in (down_local, near, far)
            ],
            out_specs=[
                pl.BlockSpec((TILE, width), lambda i, w: (0, 0)),
                pl.BlockSpec((TILE, width), lambda i, w: (jnp.maximum(i - 1, 0), 0)),
            ],
        ),
        out_shape=[
            jax.ShapeDtypeStruct((TILE, width), jnp.bfloat16),
            jax.ShapeDtypeStruct((total - TILE, width), jnp.bfloat16),
        ],
        compiler_params=pltpu.CompilerParams(vmem_limit_bytes=30 * 2**20),
        cost_estimate=pl.CostEstimate(
            flops=4 * total * units * width,
            bytes_accessed=2 * (2 * total * units + 2 * units * width + total * width),
            transcendentals=0,
        ),
    )(where, *rows, *own, other, down_local, near, far)


def line_exchange(tokens, expert_ids, combine_weights, gate_weight, up_weight, down_weight):
    node_count = lax.axis_size("node")
    local_count = lax.axis_size("local")
    planes = local_count // 2
    token_count, model_width = tokens.shape
    expert_total = node_count * planes
    gate_local, up_local, down_local = gate_weight[0], up_weight[0], down_weight[0]
    part = lax.axis_index("parts")
    node = lax.axis_index("node")
    plane = lax.axis_index("local") // 2
    side = plane // 2
    match = side == node
    end = (plane == 0) | (plane == planes - 1)
    both = ("node", "local")
    swap_half = [(i, i ^ 1) for i in range(local_count)]
    swap_two = [(0, 1), (1, 0)]

    def line_pairs(step):
        pairs = []
        for h in range(2):
            pairs += [(2 * (p + 1) + h, 2 * p + h) for p in range(planes - step)]
            pairs += [
                (local_count + 2 * (p - 1) + h, local_count + 2 * p + h) for p in range(step, planes)
            ]
        return pairs

    def back_pairs(step):
        return [(b, a) for a, b in line_pairs(step)]

    def across(x):
        return lax.ppermute(x, "node", swap_two)

    half_depth = model_width // 2
    where = jnp.stack([part * half_depth, (1 - part) * half_depth, node * planes + plane, part])
    where = where.astype(jnp.int32)

    def cut(array, offset, length, dim=0):
        begin = part * (half_depth if dim == 0 else length) + offset
        return lax.dynamic_slice_in_dim(array, begin, length, dim)

    def swap(x):
        return lax.ppermute(x, "local", swap_half)

    def relay(x):
        return lax.ppermute(x, "parts", swap_two)

    def line(x, step):
        return lax.ppermute(x, both, line_pairs(step))

    together = lax.optimization_barrier
    g0, g1, g2 = GATE_ROWS
    u0, u1, u2 = UP_ROWS
    d0, d1, d2 = (w // 2 for w in DOWN_COLUMNS)

    table = expert_weights(expert_ids, combine_weights, expert_total)
    table = jnp.pad(table, ((0, 0), (0, LANES - expert_total)))
    mine = jnp.concatenate([tokens, table], axis=1)

    gate_a = swap(cut(gate_local, 0, g0))
    theirs = across(mine)
    pair = jnp.concatenate(
        [jnp.where(node == 0, mine, theirs), jnp.where(node == 0, theirs, mine)], axis=0
    )
    pair, piece = together((pair, cut(gate_local, g0, g1)))
    got1, gate_b, gate_ax = line(pair, 1), swap(piece), relay(gate_a)
    piece = jnp.concatenate([cut(gate_local, g0 + g1, g2), cut(up_local, 0, u0)], axis=0)
    got1, gate_b, gate_ax, piece = together((got1, gate_b, gate_ax, piece))
    got2, both_c, gate_bx = line(got1, 2), swap(piece), relay(gate_b)
    other1 = across(got1)
    pieces = cut(up_local, u0, u1), cut(down_local, 0, d0, 1)
    got2, both_c, gate_bx, other1, pieces = together((got2, both_c, gate_bx, other1, pieces))
    got3, up_b, both_cx = line(got2, 3), swap(pieces[0]), relay(both_c)
    other2 = across(got2)
    slot1 = jnp.where(match, got1, other1)
    early = jnp.concatenate([pair, slot1], axis=0)
    own = [(0, -1, gate_local)], [(0, -1, up_local)]
    own_early = hidden_call(where, [early], *own)
    rest = u0 + u1
    pieces = cut(up_local, rest, u2), pieces[1]
    got3, up_b, both_cx, other2, own_early, pieces = together(
        (got3, up_b, both_cx, other2, own_early, pieces)
    )
    up_bx, up_c, down_a = relay(up_b), swap(pieces[0]), swap(pieces[1])
    other3 = across(got3)
    slot2 = jnp.where(match, got2, other2)
    slot3 = jnp.where(
        end,
        jnp.where(match, got3, other3),
        jnp.where(match, after(other1, got3), after(got1, got3)),
    )
    late = jnp.concatenate([slot2, slot3], axis=0)
    own_late = hidden_call(where, [late], *own)
    pieces = cut(down_local, 2 * d0, d1, 1), cut(down_local, 2 * (d0 + d1), d2, 1)
    up_bx, up_c, down_a, own_late, pieces = together((up_bx, up_c, down_a, own_late, pieces))
    up_cx, down_b = relay(up_c), swap(pieces[0])
    up_cx, down_a = together((up_cx, down_a))
    down_ax = relay(down_a)
    crossed = hidden_call(
        after(where, up_cx), [early, late],
        [
            (0, 0, gate_a), (g0, 0, gate_b), (g0 + g1, 0, both_c, 0, g2),
            (0, 1, gate_ax), (g0, 1, gate_bx), (g0 + g1, 1, both_cx, 0, g2),
        ],
        [
            (0, 0, both_c, g2 // u0, u0), (u0, 0, up_b), (rest, 0, up_c),
            (0, 1, both_cx, g2 // u0, u0), (u0, 1, up_bx), (rest, 1, up_cx),
        ],
    )
    down_ax, down_b, crossed, piece = together((down_ax, down_b, crossed, pieces[1]))

    def expert(first, near, far, *earlier):
        return down_call(
            after(where, *earlier), [early, late], [own_early, own_late], crossed,
            down_local, near, far, first,
        )

    def step(rows, moving, k):
        rows = rows if moving is None else add_rounded(rows, moving)
        return lax.ppermute(rows, both, back_pairs(k))

    def thirds(away, arrived):
        away = add_rounded(away, arrived)
        s1, s2, s3 = (away[i * TILE : (i + 1) * TILE] for i in range(3))
        return jnp.where(match, s1, s3), s2, s3

    def finish(home, moving):
        kept = moving.astype(jnp.float32) + home.astype(jnp.float32)
        low, high = kept[:token_count], kept[token_count:]
        sent = across(jnp.where(node == 0, high, low).astype(jnp.bfloat16))
        return (jnp.where(node == 0, low, high) + sent.astype(jnp.float32)).astype(jnp.bfloat16)

    down_bx, down_c = relay(down_b), swap(piece)
    home_a, away_a = expert(0, down_a, down_ax)
    a1, a2, a3 = thirds(away_a, across(away_a))
    moving_a = step(after(a3, down_c), None, 3)
    home_b, away_b = expert(2 * d0, down_b, down_bx, moving_a, down_c)
    down_cx = relay(down_c)
    moving_a = step(after(a2, down_bx), moving_a, 2)
    b1, b2, b3 = thirds(away_b, across(after(away_b, moving_a, down_cx)))
    moving_a = step(a1, moving_a, 1)
    moving_b = step(b3, None, 3)
    home_c, away_c = expert(2 * (d0 + d1), down_c, down_cx, b3)
    c1, c2, c3 = thirds(away_c, across(after(away_c, moving_a)))
    moving_b = step(b2, moving_b, 2)
    moving_c = step(c3, None, 3)
    moving_b = step(b1, moving_b, 1)
    moving_c = step(c2, moving_c, 2)
    moving_c = step(c1, moving_c, 1)
    results = [finish(home_a, moving_a), finish(home_b, moving_b), finish(home_c, moving_c)]
    return jnp.concatenate(results, axis=1)


def on_device(tokens, expert_ids, combine_weights, gate_weight, up_weight, down_weight):
    line = (
        lax.axis_size("parts") == 2
        and lax.axis_size("node") == 2
        and lax.axis_size("local") == 8
        and tokens.shape == (128, 3584)
        and gate_weight.shape[2] == 512
    )
    form = line_exchange if line else packed_exchange
    return form(tokens, expert_ids, combine_weights, gate_weight, up_weight, down_weight)


def solution(mesh):
    in_specs = (
        P(("parts", "node", "local"), None),
        P(("parts", "node", "local"), None),
        P(("parts", "node", "local"), None),
        P(("node", "local"), None, None),
        P(("node", "local"), None, None),
        P(("node", "local"), None, None),
    )
    out_specs = P(("parts", "node", "local"), None)
    return jax.shard_map(
        on_device, mesh=mesh, in_specs=in_specs, out_specs=out_specs, check_vma=False
    )
```

```python
import functools

import jax
import jax.numpy as jnp
from jax import lax
from jax.experimental import pallas as pl
from jax.experimental.pallas import tpu as pltpu
from jax.sharding import PartitionSpec as P

TILE = 256
LANES = 128
STEPS = 4
GATE_ROWS = (512, 768, 512)
UP_ROWS = (512, 1024, 256)
DOWN_COLUMNS = (1024, 1280, 1280)


def slot_tables(routes, first_expert, expert_count, capacity, expert_total):
    options = jnp.arange(expert_total, dtype=jnp.int32)
    matches = routes[:, :, None] == options[None, None, :]
    counts = jnp.sum(matches.astype(jnp.int32), axis=1)
    before = jnp.cumsum(counts, axis=0) - counts
    rank_in = jnp.sum(jnp.where(matches, before[:, None, :], 0), axis=2)
    local_index = routes - first_expert
    inside = (local_index >= 0) & (local_index < expert_count)
    return (local_index * capacity + rank_in, inside)


def dispatch_matrix(slot_index, inside, total_slots):
    positions = jnp.arange(total_slots, dtype=jnp.int32)
    matches = (slot_index[None, :, :] == positions[:, None, None]) & inside[None, :, :]
    return jnp.sum(matches.astype(jnp.float32), axis=2).astype(jnp.bfloat16)


def weight_matrix(slot_index, inside, weights, total_slots):
    positions = jnp.arange(total_slots, dtype=jnp.int32)
    matches = (slot_index[:, :, None] == positions[None, None, :]) & inside[:, :, None]
    spread = jnp.where(matches, weights.astype(jnp.float32)[:, :, None], 0.0)
    return jnp.sum(spread, axis=1).astype(jnp.bfloat16)


def apply_expert(rows, gate_local, up_local, down_local):
    gate_value = jnp.dot(rows, gate_local, preferred_element_type=jnp.float32)
    up_value = jnp.dot(rows, up_local, preferred_element_type=jnp.float32)
    hidden = (jax.nn.silu(gate_value) * up_value).astype(jnp.bfloat16)
    return jnp.dot(hidden, down_local, preferred_element_type=jnp.float32).astype(jnp.bfloat16)


def packed_exchange(tokens, expert_ids, combine_weights, gate_weight, up_weight, down_weight):
    node_count = lax.axis_size("node")
    local_count = lax.axis_size("local")
    per_node = local_count // 2
    expert_total = node_count * per_node
    token_count = tokens.shape[0]
    model_width = tokens.shape[1]
    top_count = expert_ids.shape[1]
    capacity = token_count * top_count * 5 // (4 * expert_total)
    gate_local = gate_weight[0]
    up_local = up_weight[0]
    down_local = down_weight[0]
    rows_all, weights_all = (
        lax.all_gather(tokens, "node", axis=0, tiled=True),
        lax.all_gather(combine_weights, "node", axis=0, tiled=True),
    )
    routes_all = lax.all_gather(expert_ids, "node", axis=0, tiled=True)
    first_expert = lax.axis_index("node") * per_node
    total_slots = per_node * capacity
    routes_blocks = routes_all.reshape(node_count, token_count, top_count)
    slot_index, inside = jax.vmap(
        lambda routes: slot_tables(routes, first_expert, per_node, capacity, expert_total)
    )(routes_blocks)
    placing = jax.vmap(lambda slots, marks: dispatch_matrix(slots, marks, total_slots))(
        slot_index, inside
    )
    row_blocks = rows_all.reshape(node_count, token_count, model_width)
    packed = jnp.einsum(
        "bst,btd->bsd", placing, row_blocks, preferred_element_type=jnp.float32
    ).astype(jnp.bfloat16)
    packed = packed.reshape(node_count, per_node, capacity, model_width).transpose(1, 0, 2, 3)
    outgoing = jnp.broadcast_to(packed[:, None], (per_node, 2, node_count, capacity, model_width))
    outgoing = outgoing.reshape(local_count, node_count * capacity, model_width)
    rows = lax.all_to_all(outgoing, "local", split_axis=0, concat_axis=0, tiled=True)
    in_shape = rows.shape
    flat_rows = rows.reshape(-1, model_width)
    returned = lax.all_to_all(
        apply_expert(flat_rows, gate_local, up_local, down_local).reshape(in_shape),
        "local",
        split_axis=0,
        concat_axis=0,
        tiled=True,
    )
    returned = returned.reshape(per_node, 2, node_count, capacity, model_width).astype(jnp.float32)
    results = (returned[:, 0] + returned[:, 1]).astype(jnp.bfloat16)
    by_block = results.transpose(1, 0, 2, 3).reshape(node_count, total_slots, model_width)
    weight_blocks = weights_all.reshape(node_count, token_count, top_count)
    mixing = jax.vmap(
        lambda slots, marks, weights: weight_matrix(slots, marks, weights, total_slots)
    )(slot_index, inside, weight_blocks)
    contrib = jnp.einsum(
        "bts,bsd->btd", mixing, by_block, preferred_element_type=jnp.float32
    ).astype(jnp.bfloat16)
    contrib = lax.optimization_barrier(contrib)
    summed_out = lax.psum_scatter(
        contrib.astype(jnp.float32).astype(jnp.bfloat16), "node", scatter_dimension=0, tiled=True
    ).astype(jnp.float32)
    return summed_out[0].astype(jnp.bfloat16)


def expert_weights(expert_ids, combine_weights, expert_total):
    options = jnp.arange(expert_total, dtype=jnp.int32)
    matches = expert_ids[:, :, None] == options[None, None, :]
    spread = jnp.where(matches, combine_weights.astype(jnp.float32)[:, :, None], 0.0)
    return jnp.sum(spread, axis=1).astype(jnp.bfloat16)


def add_rounded(first, second):
    return (first.astype(jnp.float32) + second.astype(jnp.float32)).astype(jnp.bfloat16)


def after(x, *earlier):
    return lax.optimization_barrier((x, *earlier))[0] if earlier else x


def dot32(a, b):
    return jnp.dot(a, b, preferred_element_type=jnp.float32)


def hidden_kernel(batches, gate_pieces, up_pieces, where_ref, *refs):
    rows_refs = refs[:batches]
    gates = refs[batches : batches + len(gate_pieces)]
    ups = refs[batches + len(gate_pieces) : -1]
    out_ref = refs[-1]
    step = pl.program_id(0)
    steps_each = pl.num_programs(0) // batches

    def product(rows, pieces, weights):
        total = None
        for (offset, kind), w in zip(pieces, weights):
            if kind < 0:
                columns = slice(offset, offset + w.shape[0])
            else:
                columns = pl.ds(pl.multiple_of(where_ref[kind] + offset, LANES), w.shape[0])
            value = dot32(rows[:, columns], w[...])
            total = value if total is None else total + value
        return total

    def work(rows):
        gate_value = product(rows, gate_pieces, gates)
        up_value = product(rows, up_pieces, ups)
        out_ref[...] = (gate_value / (1.0 + jnp.exp(-gate_value)) * up_value).astype(jnp.bfloat16)

    for b in range(batches):
        pl.when(step // steps_each == b)(functools.partial(work, rows_refs[b]))


def hidden_call(where, rows, gate_parts, up_parts):
    gate_pieces, up_pieces = [p[:2] for p in gate_parts], [p[:2] for p in up_parts]
    gates, ups = [p[2] for p in gate_parts], [p[2] for p in up_parts]
    blocks = [(p[3], p[4]) if len(p) > 3 else (0, p[2].shape[0]) for p in gate_parts + up_parts]
    batches = len(rows)
    steps_each = rows[0].shape[0] // TILE
    width = rows[0].shape[1]
    units = gates[0].shape[1]

    def rows_map(b):
        return lambda i, w: (jnp.clip(i - b * steps_each, 0, steps_each - 1), 0)

    total = batches * steps_each * TILE
    depth = width - LANES
    once = pl.Buffered(1)

    def block_map(block):
        return lambda i, w: (block, 0)

    return pl.pallas_call(
        functools.partial(hidden_kernel, batches, gate_pieces, up_pieces),
        grid_spec=pltpu.PrefetchScalarGridSpec(
            num_scalar_prefetch=1,
            grid=(batches * steps_each,),
            in_specs=[pl.BlockSpec((TILE, width), rows_map(b)) for b in range(batches)]
            + [
                pl.BlockSpec((length, units), block_map(block), pipeline_mode=once)
                for block, length in blocks
            ],
            out_specs=pl.BlockSpec((TILE, units), lambda i, w: (i, 0)),
        ),
        out_shape=jax.ShapeDtypeStruct((total, units), jnp.bfloat16),
        compiler_params=pltpu.CompilerParams(vmem_limit_bytes=30 * 2**20),
        cost_estimate=pl.CostEstimate(
            flops=4 * total * depth * units,
            bytes_accessed=2 * (total * width + 2 * depth * units + total * units),
            transcendentals=total * units,
        ),
    )(where, *rows, *gates, *ups)


def down_kernel(batches, first, width, where_ref, *refs):
    spread_refs = refs[:batches]
    own_refs = refs[batches : 2 * batches]
    other_ref, down_ref, near_ref, far_ref, home_ref, away_ref = refs[2 * batches :]
    step = pl.program_id(0)
    half = width // 2

    def work(spread, own, out_ref):
        chosen = lax.broadcasted_iota(jnp.int32, spread.shape, 1) == where_ref[2]
        scale = jnp.sum(jnp.where(chosen, spread[...].astype(jnp.float32), 0.0), axis=1, keepdims=True)
        for piece, slot in ((near_ref, where_ref[3]), (far_ref, 1 - where_ref[3])):
            source = pl.ds(pl.multiple_of(first + slot * half, LANES), half)
            target = pl.ds(pl.multiple_of(slot * half, LANES), half)
            value = dot32(own[...], down_ref[:, source]) + dot32(other_ref[...], piece[...])
            out_ref[:, target] = (value * scale).astype(jnp.bfloat16)

    for i in range(STEPS):
        b = i * batches // STEPS
        pl.when(step == i)(
            functools.partial(work, spread_refs[b], own_refs[b], home_ref if i == 0 else away_ref)
        )


def down_call(where, rows, own, other, down_local, near, far, first):
    batches = len(rows)
    steps_each = rows[0].shape[0] // TILE
    units = down_local.shape[0]
    width = 2 * near.shape[1]
    last = rows[0].shape[1] // LANES - 1

    def tile_map(b, column):
        return lambda i, w: (jnp.clip(i - b * steps_each, 0, steps_each - 1), column)

    once = pl.Buffered(1)
    total = batches * steps_each * TILE
    return pl.pallas_call(
        functools.partial(down_kernel, batches, first, width),
        grid_spec=pltpu.PrefetchScalarGridSpec(
            num_scalar_prefetch=1,
            grid=(batches * steps_each,),
            in_specs=[pl.BlockSpec((TILE, LANES), tile_map(b, last)) for b in range(batches)]
            + [pl.BlockSpec((TILE, units), tile_map(b, 0)) for b in range(batches)]
            + [pl.BlockSpec((TILE, units), lambda i, w: (i, 0))]
            + [
                pl.BlockSpec(a.shape, lambda i, w: (0, 0), pipeline_mode=once)
                for a in (down_local, near, far)
            ],
            out_specs=[
                pl.BlockSpec((TILE, width), lambda i, w: (0, 0)),
                pl.BlockSpec((TILE, width), lambda i, w: (jnp.maximum(i - 1, 0), 0)),
            ],
        ),
        out_shape=[
            jax.ShapeDtypeStruct((TILE, width), jnp.bfloat16),
            jax.ShapeDtypeStruct((total - TILE, width), jnp.bfloat16),
        ],
        compiler_params=pltpu.CompilerParams(vmem_limit_bytes=30 * 2**20),
        cost_estimate=pl.CostEstimate(
            flops=4 * total * units * width,
            bytes_accessed=2 * (2 * total * units + 2 * units * width + total * width),
            transcendentals=0,
        ),
    )(where, *rows, *own, other, down_local, near, far)


def line_exchange(tokens, expert_ids, combine_weights, gate_weight, up_weight, down_weight):
    node_count = lax.axis_size("node")
    local_count = lax.axis_size("local")
    planes = local_count // 2
    token_count, model_width = tokens.shape
    expert_total = node_count * planes
    gate_local, up_local, down_local = gate_weight[0], up_weight[0], down_weight[0]
    part = lax.axis_index("parts")
    node = lax.axis_index("node")
    plane = lax.axis_index("local") // 2
    side = plane // 2
    match = side == node
    end = (plane == 0) | (plane == planes - 1)
    both = ("node", "local")
    swap_half = [(i, i ^ 1) for i in range(local_count)]
    swap_two = [(0, 1), (1, 0)]

    def line_pairs(step):
        pairs = []
        for h in range(2):
            pairs += [(2 * (p + 1) + h, 2 * p + h) for p in range(planes - step)]
            pairs += [
                (local_count + 2 * (p - 1) + h, local_count + 2 * p + h) for p in range(step, planes)
            ]
        return pairs

    def back_pairs(step):
        return [(b, a) for a, b in line_pairs(step)]

    def across(x):
        return lax.ppermute(x, "node", swap_two)

    half_depth = model_width // 2
    where = jnp.stack([part * half_depth, (1 - part) * half_depth, node * planes + plane, part])
    where = where.astype(jnp.int32)

    def cut(array, offset, length, dim=0):
        begin = part * (half_depth if dim == 0 else length) + offset
        return lax.dynamic_slice_in_dim(array, begin, length, dim)

    def swap(x):
        return lax.ppermute(x, "local", swap_half)

    def relay(x):
        return lax.ppermute(x, "parts", swap_two)

    def line(x, step):
        return lax.ppermute(x, both, line_pairs(step))

    together = lax.optimization_barrier
    g0, g1, g2 = GATE_ROWS
    u0, u1, u2 = UP_ROWS
    d0, d1, d2 = (w // 2 for w in DOWN_COLUMNS)

    table = expert_weights(expert_ids, combine_weights, expert_total)
    table = jnp.pad(table, ((0, 0), (0, LANES - expert_total)))
    mine = jnp.concatenate([tokens, table], axis=1)

    gate_a = swap(cut(gate_local, 0, g0))
    theirs = across(mine)
    pair = jnp.concatenate(
        [jnp.where(node == 0, mine, theirs), jnp.where(node == 0, theirs, mine)], axis=0
    )
    pair, piece = together((pair, cut(gate_local, g0, g1)))
    got1, gate_b, gate_ax = line(pair, 1), swap(piece), relay(gate_a)
    piece = jnp.concatenate([cut(gate_local, g0 + g1, g2), cut(up_local, 0, u0)], axis=0)
    got1, gate_b, gate_ax, piece = together((got1, gate_b, gate_ax, piece))
    got2, both_c, gate_bx = line(got1, 2), swap(piece), relay(gate_b)
    other1 = across(got1)
    pieces = cut(up_local, u0, u1), cut(down_local, 0, d0, 1)
    got2, both_c, gate_bx, other1, pieces = together((got2, both_c, gate_bx, other1, pieces))
    got3, up_b, both_cx = line(got2, 3), swap(pieces[0]), relay(both_c)
    other2 = across(got2)
    slot1 = jnp.where(match, got1, other1)
    early = jnp.concatenate([pair, slot1], axis=0)
    own = [(0, -1, gate_local)], [(0, -1, up_local)]
    own_early = hidden_call(where, [early], *own)
    rest = u0 + u1
    piece = jnp.concatenate([up_local[rest:half_depth], up_local[half_depth + rest :]], axis=0)
    pieces = piece, pieces[1]
    got3, up_b, both_cx, other2, own_early, pieces = together(
        (got3, up_b, both_cx, other2, own_early, pieces)
    )
    up_bx, up_c, down_a = relay(up_b), swap(pieces[0]), swap(pieces[1])
    other3 = across(got3)
    slot2 = jnp.where(match, got2, other2)
    slot3 = jnp.where(
        end,
        jnp.where(match, got3, other3),
        jnp.where(match, after(other1, got3), after(got1, got3)),
    )
    late = jnp.concatenate([slot2, slot3], axis=0)
    own_late = hidden_call(where, [late], *own)
    pieces = cut(down_local, 2 * d0, d1, 1), cut(down_local, 2 * (d0 + d1), d2, 1)
    up_bx, up_c, down_a, own_late, pieces = together((up_bx, up_c, down_a, own_late, pieces))
    down_ax, down_b = relay(down_a), swap(pieces[0])
    crossed = hidden_call(
        where, [early, late],
        [
            (0, 0, gate_a), (g0, 0, gate_b), (g0 + g1, 0, both_c, 0, g2),
            (0, 1, gate_ax), (g0, 1, gate_bx), (g0 + g1, 1, both_cx, 0, g2),
        ],
        [
            (0, 0, both_c, g2 // u0, u0), (u0, 0, up_b),
            (0, 1, both_cx, g2 // u0, u0), (u0, 1, up_bx),
            (rest, -1, up_c, 0, u2), (half_depth + rest, -1, up_c, 1, u2),
        ],
    )
    down_ax, down_b, crossed, piece = together((down_ax, down_b, crossed, pieces[1]))

    def expert(first, near, far, *earlier):
        return down_call(
            after(where, *earlier), [early, late], [own_early, own_late], crossed,
            down_local, near, far, first,
        )

    def step(rows, moving, k):
        rows = rows if moving is None else add_rounded(rows, moving)
        return lax.ppermute(rows, both, back_pairs(k))

    def thirds(away, arrived):
        away = add_rounded(away, arrived)
        s1, s2, s3 = (away[i * TILE : (i + 1) * TILE] for i in range(3))
        return jnp.where(match, s1, s3), s2, s3

    def finish(home, moving):
        kept = moving.astype(jnp.float32) + home.astype(jnp.float32)
        low, high = kept[:token_count], kept[token_count:]
        sent = across(jnp.where(node == 0, high, low).astype(jnp.bfloat16))
        return (jnp.where(node == 0, low, high) + sent.astype(jnp.float32)).astype(jnp.bfloat16)

    down_bx, down_c = relay(down_b), swap(piece)
    home_a, away_a = expert(0, down_a, down_ax)
    a1, a2, a3 = thirds(away_a, across(away_a))
    moving_a = step(a3, None, 3)
    home_b, away_b = expert(2 * d0, down_b, down_bx, moving_a, down_c)
    down_cx = relay(down_c)
    moving_a = step(after(a2, down_bx, down_c), moving_a, 2)
    b1, b2, b3 = thirds(away_b, across(after(away_b, moving_a, down_cx)))
    moving_a = step(a1, moving_a, 1)
    moving_b = step(b3, None, 3)
    home_c, away_c = expert(2 * (d0 + d1), down_c, down_cx, b3)
    c1, c2, c3 = thirds(away_c, across(after(away_c, moving_a)))
    moving_b = step(b2, moving_b, 2)
    moving_c = step(c3, None, 3)
    moving_b = step(b1, moving_b, 1)
    moving_c = step(c2, moving_c, 2)
    moving_c = step(c1, moving_c, 1)
    results = [finish(home_a, moving_a), finish(home_b, moving_b), finish(home_c, moving_c)]
    return jnp.concatenate(results, axis=1)


def on_device(tokens, expert_ids, combine_weights, gate_weight, up_weight, down_weight):
    line = (
        lax.axis_size("parts") == 2
        and lax.axis_size("node") == 2
        and lax.axis_size("local") == 8
        and tokens.shape == (128, 3584)
        and gate_weight.shape[2] == 512
    )
    form = line_exchange if line else packed_exchange
    return form(tokens, expert_ids, combine_weights, gate_weight, up_weight, down_weight)


def solution(mesh):
    in_specs = (
        P(("parts", "node", "local"), None),
        P(("parts", "node", "local"), None),
        P(("parts", "node", "local"), None),
        P(("node", "local"), None, None),
        P(("node", "local"), None, None),
        P(("node", "local"), None, None),
    )
    out_specs = P(("parts", "node", "local"), None)
    return jax.shard_map(
        on_device, mesh=mesh, in_specs=in_specs, out_specs=out_specs, check_vma=False
    )
```

```python
import functools

import jax
import jax.numpy as jnp
from jax import lax
from jax.experimental import pallas as pl
from jax.experimental.pallas import tpu as pltpu
from jax.sharding import PartitionSpec as P

TILE = 256
LANES = 128
STEPS = 4
GATE_ROWS = (512, 768, 512)
UP_ROWS = (512, 1024, 256)
DOWN_COLUMNS = (1024, 1280, 1280)


def slot_tables(routes, first_expert, expert_count, capacity, expert_total):
    options = jnp.arange(expert_total, dtype=jnp.int32)
    matches = routes[:, :, None] == options[None, None, :]
    counts = jnp.sum(matches.astype(jnp.int32), axis=1)
    before = jnp.cumsum(counts, axis=0) - counts
    rank_in = jnp.sum(jnp.where(matches, before[:, None, :], 0), axis=2)
    local_index = routes - first_expert
    inside = (local_index >= 0) & (local_index < expert_count)
    return (local_index * capacity + rank_in, inside)


def dispatch_matrix(slot_index, inside, total_slots):
    positions = jnp.arange(total_slots, dtype=jnp.int32)
    matches = (slot_index[None, :, :] == positions[:, None, None]) & inside[None, :, :]
    return jnp.sum(matches.astype(jnp.float32), axis=2).astype(jnp.bfloat16)


def weight_matrix(slot_index, inside, weights, total_slots):
    positions = jnp.arange(total_slots, dtype=jnp.int32)
    matches = (slot_index[:, :, None] == positions[None, None, :]) & inside[:, :, None]
    spread = jnp.where(matches, weights.astype(jnp.float32)[:, :, None], 0.0)
    return jnp.sum(spread, axis=1).astype(jnp.bfloat16)


def apply_expert(rows, gate_local, up_local, down_local):
    gate_value = jnp.dot(rows, gate_local, preferred_element_type=jnp.float32)
    up_value = jnp.dot(rows, up_local, preferred_element_type=jnp.float32)
    hidden = (jax.nn.silu(gate_value) * up_value).astype(jnp.bfloat16)
    return jnp.dot(hidden, down_local, preferred_element_type=jnp.float32).astype(jnp.bfloat16)


def packed_exchange(tokens, expert_ids, combine_weights, gate_weight, up_weight, down_weight):
    node_count = lax.axis_size("node")
    local_count = lax.axis_size("local")
    per_node = local_count // 2
    expert_total = node_count * per_node
    token_count = tokens.shape[0]
    model_width = tokens.shape[1]
    top_count = expert_ids.shape[1]
    capacity = token_count * top_count * 5 // (4 * expert_total)
    gate_local = gate_weight[0]
    up_local = up_weight[0]
    down_local = down_weight[0]
    rows_all, weights_all = (
        lax.all_gather(tokens, "node", axis=0, tiled=True),
        lax.all_gather(combine_weights, "node", axis=0, tiled=True),
    )
    routes_all = lax.all_gather(expert_ids, "node", axis=0, tiled=True)
    first_expert = lax.axis_index("node") * per_node
    total_slots = per_node * capacity
    routes_blocks = routes_all.reshape(node_count, token_count, top_count)
    slot_index, inside = jax.vmap(
        lambda routes: slot_tables(routes, first_expert, per_node, capacity, expert_total)
    )(routes_blocks)
    placing = jax.vmap(lambda slots, marks: dispatch_matrix(slots, marks, total_slots))(
        slot_index, inside
    )
    row_blocks = rows_all.reshape(node_count, token_count, model_width)
    packed = jnp.einsum(
        "bst,btd->bsd", placing, row_blocks, preferred_element_type=jnp.float32
    ).astype(jnp.bfloat16)
    packed = packed.reshape(node_count, per_node, capacity, model_width).transpose(1, 0, 2, 3)
    outgoing = jnp.broadcast_to(packed[:, None], (per_node, 2, node_count, capacity, model_width))
    outgoing = outgoing.reshape(local_count, node_count * capacity, model_width)
    rows = lax.all_to_all(outgoing, "local", split_axis=0, concat_axis=0, tiled=True)
    in_shape = rows.shape
    flat_rows = rows.reshape(-1, model_width)
    returned = lax.all_to_all(
        apply_expert(flat_rows, gate_local, up_local, down_local).reshape(in_shape),
        "local",
        split_axis=0,
        concat_axis=0,
        tiled=True,
    )
    returned = returned.reshape(per_node, 2, node_count, capacity, model_width).astype(jnp.float32)
    results = (returned[:, 0] + returned[:, 1]).astype(jnp.bfloat16)
    by_block = results.transpose(1, 0, 2, 3).reshape(node_count, total_slots, model_width)
    weight_blocks = weights_all.reshape(node_count, token_count, top_count)
    mixing = jax.vmap(
        lambda slots, marks, weights: weight_matrix(slots, marks, weights, total_slots)
    )(slot_index, inside, weight_blocks)
    contrib = jnp.einsum(
        "bts,bsd->btd", mixing, by_block, preferred_element_type=jnp.float32
    ).astype(jnp.bfloat16)
    contrib = lax.optimization_barrier(contrib)
    summed_out = lax.psum_scatter(
        contrib.astype(jnp.float32).astype(jnp.bfloat16), "node", scatter_dimension=0, tiled=True
    ).astype(jnp.float32)
    return summed_out[0].astype(jnp.bfloat16)


def expert_weights(expert_ids, combine_weights, expert_total):
    options = jnp.arange(expert_total, dtype=jnp.int32)
    matches = expert_ids[:, :, None] == options[None, None, :]
    spread = jnp.where(matches, combine_weights.astype(jnp.float32)[:, :, None], 0.0)
    return jnp.sum(spread, axis=1).astype(jnp.bfloat16)


def add_rounded(first, second):
    return (first.astype(jnp.float32) + second.astype(jnp.float32)).astype(jnp.bfloat16)


def after(x, *earlier):
    return lax.optimization_barrier((x, *earlier))[0] if earlier else x


def dot32(a, b):
    return jnp.dot(a, b, preferred_element_type=jnp.float32)


def hidden_kernel(batches, gate_pieces, up_pieces, where_ref, *refs):
    rows_refs = refs[:batches]
    gates = refs[batches : batches + len(gate_pieces)]
    ups = refs[batches + len(gate_pieces) : -1]
    out_ref = refs[-1]
    step = pl.program_id(0)
    steps_each = pl.num_programs(0) // batches

    def product(rows, pieces, weights):
        total = None
        for (offset, kind), w in zip(pieces, weights):
            if kind < 0:
                columns = slice(offset, offset + w.shape[0])
            else:
                columns = pl.ds(pl.multiple_of(where_ref[kind] + offset, LANES), w.shape[0])
            value = dot32(rows[:, columns], w[...])
            total = value if total is None else total + value
        return total

    def work(rows):
        gate_value = product(rows, gate_pieces, gates)
        up_value = product(rows, up_pieces, ups)
        out_ref[...] = (gate_value / (1.0 + jnp.exp(-gate_value)) * up_value).astype(jnp.bfloat16)

    for b in range(batches):
        pl.when(step // steps_each == b)(functools.partial(work, rows_refs[b]))


def hidden_call(where, rows, gate_parts, up_parts):
    gate_pieces, up_pieces = [p[:2] for p in gate_parts], [p[:2] for p in up_parts]
    gates, ups = [p[2] for p in gate_parts], [p[2] for p in up_parts]
    blocks = [(p[3], p[4]) if len(p) > 3 else (0, p[2].shape[0]) for p in gate_parts + up_parts]
    batches = len(rows)
    steps_each = rows[0].shape[0] // TILE
    width = rows[0].shape[1]
    units = gates[0].shape[1]

    def rows_map(b):
        return lambda i, w: (jnp.clip(i - b * steps_each, 0, steps_each - 1), 0)

    total = batches * steps_each * TILE
    depth = width - LANES
    once = pl.Buffered(1)

    def block_map(block):
        return lambda i, w: (block, 0)

    return pl.pallas_call(
        functools.partial(hidden_kernel, batches, gate_pieces, up_pieces),
        grid_spec=pltpu.PrefetchScalarGridSpec(
            num_scalar_prefetch=1,
            grid=(batches * steps_each,),
            in_specs=[pl.BlockSpec((TILE, width), rows_map(b)) for b in range(batches)]
            + [
                pl.BlockSpec((length, units), block_map(block), pipeline_mode=once)
                for block, length in blocks
            ],
            out_specs=pl.BlockSpec((TILE, units), lambda i, w: (i, 0)),
        ),
        out_shape=jax.ShapeDtypeStruct((total, units), jnp.bfloat16),
        compiler_params=pltpu.CompilerParams(vmem_limit_bytes=30 * 2**20),
        cost_estimate=pl.CostEstimate(
            flops=4 * total * depth * units,
            bytes_accessed=2 * (total * width + 2 * depth * units + total * units),
            transcendentals=total * units,
        ),
    )(where, *rows, *gates, *ups)


def down_kernel(batches, first, width, where_ref, *refs):
    spread_refs = refs[:batches]
    own_refs = refs[batches : 2 * batches]
    other_ref, down_ref, near_ref, far_ref, home_ref, away_ref = refs[2 * batches :]
    step = pl.program_id(0)
    half = width // 2

    def work(spread, own, out_ref):
        chosen = lax.broadcasted_iota(jnp.int32, spread.shape, 1) == where_ref[2]
        scale = jnp.sum(jnp.where(chosen, spread[...].astype(jnp.float32), 0.0), axis=1, keepdims=True)
        for piece, slot in ((near_ref, where_ref[3]), (far_ref, 1 - where_ref[3])):
            source = pl.ds(pl.multiple_of(first + slot * half, LANES), half)
            target = pl.ds(pl.multiple_of(slot * half, LANES), half)
            value = dot32(own[...], down_ref[:, source]) + dot32(other_ref[...], piece[...])
            out_ref[:, target] = (value * scale).astype(jnp.bfloat16)

    for i in range(STEPS):
        b = i * batches // STEPS
        pl.when(step == i)(
            functools.partial(work, spread_refs[b], own_refs[b], home_ref if i == 0 else away_ref)
        )


def down_call(where, rows, own, other, down_local, near, far, first):
    batches = len(rows)
    steps_each = rows[0].shape[0] // TILE
    units = down_local.shape[0]
    width = 2 * near.shape[1]
    last = rows[0].shape[1] // LANES - 1

    def tile_map(b, column):
        return lambda i, w: (jnp.clip(i - b * steps_each, 0, steps_each - 1), column)

    once = pl.Buffered(1)
    total = batches * steps_each * TILE
    return pl.pallas_call(
        functools.partial(down_kernel, batches, first, width),
        grid_spec=pltpu.PrefetchScalarGridSpec(
            num_scalar_prefetch=1,
            grid=(batches * steps_each,),
            in_specs=[pl.BlockSpec((TILE, LANES), tile_map(b, last)) for b in range(batches)]
            + [pl.BlockSpec((TILE, units), tile_map(b, 0)) for b in range(batches)]
            + [pl.BlockSpec((TILE, units), lambda i, w: (i, 0))]
            + [
                pl.BlockSpec(a.shape, lambda i, w: (0, 0), pipeline_mode=once)
                for a in (down_local, near, far)
            ],
            out_specs=[
                pl.BlockSpec((TILE, width), lambda i, w: (0, 0)),
                pl.BlockSpec((TILE, width), lambda i, w: (jnp.maximum(i - 1, 0), 0)),
            ],
        ),
        out_shape=[
            jax.ShapeDtypeStruct((TILE, width), jnp.bfloat16),
            jax.ShapeDtypeStruct((total - TILE, width), jnp.bfloat16),
        ],
        compiler_params=pltpu.CompilerParams(vmem_limit_bytes=30 * 2**20),
        cost_estimate=pl.CostEstimate(
            flops=4 * total * units * width,
            bytes_accessed=2 * (2 * total * units + 2 * units * width + total * width),
            transcendentals=0,
        ),
    )(where, *rows, *own, other, down_local, near, far)


def line_exchange(tokens, expert_ids, combine_weights, gate_weight, up_weight, down_weight):
    node_count = lax.axis_size("node")
    local_count = lax.axis_size("local")
    planes = local_count // 2
    token_count, model_width = tokens.shape
    expert_total = node_count * planes
    gate_local, up_local, down_local = gate_weight[0], up_weight[0], down_weight[0]
    part = lax.axis_index("parts")
    node = lax.axis_index("node")
    plane = lax.axis_index("local") // 2
    side = plane // 2
    match = side == node
    end = (plane == 0) | (plane == planes - 1)
    both = ("node", "local")
    swap_half = [(i, i ^ 1) for i in range(local_count)]
    swap_two = [(0, 1), (1, 0)]

    def line_pairs(step):
        pairs = []
        for h in range(2):
            pairs += [(2 * (p + 1) + h, 2 * p + h) for p in range(planes - step)]
            pairs += [
                (local_count + 2 * (p - 1) + h, local_count + 2 * p + h) for p in range(step, planes)
            ]
        return pairs

    def back_pairs(step):
        return [(b, a) for a, b in line_pairs(step)]

    def across(x):
        return lax.ppermute(x, "node", swap_two)

    half_depth = model_width // 2
    where = jnp.stack([part * half_depth, (1 - part) * half_depth, node * planes + plane, part])
    where = where.astype(jnp.int32)

    def cut(array, offset, length, dim=0):
        begin = part * (half_depth if dim == 0 else length) + offset
        return lax.dynamic_slice_in_dim(array, begin, length, dim)

    def swap(x):
        return lax.ppermute(x, "local", swap_half)

    def relay(x):
        return lax.ppermute(x, "parts", swap_two)

    def line(x, step):
        return lax.ppermute(x, both, line_pairs(step))

    together = lax.optimization_barrier
    g0, g1, g2 = GATE_ROWS
    u0, u1, u2 = UP_ROWS
    d0, d1, d2 = (w // 2 for w in DOWN_COLUMNS)

    table = expert_weights(expert_ids, combine_weights, expert_total)
    table = jnp.pad(table, ((0, 0), (0, LANES - expert_total)))
    mine = jnp.concatenate([tokens, table], axis=1)

    gate_a = swap(cut(gate_local, 0, g0))
    theirs = across(mine)
    pair = jnp.concatenate(
        [jnp.where(node == 0, mine, theirs), jnp.where(node == 0, theirs, mine)], axis=0
    )
    pair, piece = together((pair, cut(gate_local, g0, g1)))
    got1, gate_b, gate_ax = line(pair, 1), swap(piece), relay(gate_a)
    piece = jnp.concatenate([cut(gate_local, g0 + g1, g2), cut(up_local, 0, u0)], axis=0)
    got1, gate_b, gate_ax, piece = together((got1, gate_b, gate_ax, piece))
    got2, both_c, gate_bx = line(got1, 2), swap(piece), relay(gate_b)
    other1 = across(got1)
    pieces = cut(up_local, u0, u1), cut(down_local, 0, d0, 1)
    got2, both_c, gate_bx, other1, pieces = together((got2, both_c, gate_bx, other1, pieces))
    got3, up_b, both_cx = line(got2, 3), swap(pieces[0]), relay(both_c)
    other2 = across(got2)
    slot1 = jnp.where(match, got1, other1)
    early = jnp.concatenate([pair, slot1], axis=0)
    own = [(0, -1, gate_local)], [(0, -1, up_local)]
    own_early = hidden_call(where, [early], *own)
    rest = u0 + u1
    piece = jnp.concatenate([up_local[rest:half_depth], up_local[half_depth + rest :]], axis=0)
    pieces = piece, pieces[1], cut(down_local, 2 * d0, d1, 1), cut(down_local, 2 * (d0 + d1), d2, 1)
    got3, up_b, both_cx, other2, own_early, pieces = together(
        (got3, up_b, both_cx, other2, own_early, pieces)
    )
    up_bx, up_c, down_a = relay(up_b), swap(pieces[0]), swap(pieces[1])
    other3 = across(got3)
    slot2 = jnp.where(match, got2, other2)
    slot3 = jnp.where(
        end,
        jnp.where(match, got3, other3),
        jnp.where(match, after(other1, got3), after(got1, got3)),
    )
    late = jnp.concatenate([slot2, slot3], axis=0)
    own_late = hidden_call(where, [late], *own)
    up_bx, up_c, down_a, own_late, pieces = together((up_bx, up_c, down_a, own_late, pieces))
    down_ax, down_b = relay(down_a), swap(pieces[2])
    crossed = hidden_call(
        where, [early, late],
        [
            (0, 0, gate_a), (g0, 0, gate_b), (g0 + g1, 0, both_c, 0, g2),
            (0, 1, gate_ax), (g0, 1, gate_bx), (g0 + g1, 1, both_cx, 0, g2),
        ],
        [
            (0, 0, both_c, g2 // u0, u0), (u0, 0, up_b),
            (0, 1, both_cx, g2 // u0, u0), (u0, 1, up_bx),
            (rest, -1, up_c, 0, u2), (half_depth + rest, -1, up_c, 1, u2),
        ],
    )
    down_ax, down_b, crossed, piece = together((down_ax, down_b, crossed, pieces[3]))

    def expert(first, near, far, *earlier):
        return down_call(
            after(where, *earlier), [early, late], [own_early, own_late], crossed,
            down_local, near, far, first,
        )

    def step(rows, moving, k):
        rows = rows if moving is None else add_rounded(rows, moving)
        return lax.ppermute(rows, both, back_pairs(k))

    def thirds(away, arrived):
        away = add_rounded(away, arrived)
        s1, s2, s3 = (away[i * TILE : (i + 1) * TILE] for i in range(3))
        return jnp.where(match, s1, s3), s2, s3

    def finish(home, moving):
        kept = moving.astype(jnp.float32) + home.astype(jnp.float32)
        low, high = kept[:token_count], kept[token_count:]
        sent = across(jnp.where(node == 0, high, low).astype(jnp.bfloat16))
        return (jnp.where(node == 0, low, high) + sent.astype(jnp.float32)).astype(jnp.bfloat16)

    down_bx, down_c = relay(down_b), swap(piece)
    home_a, away_a = expert(0, down_a, down_ax)
    a1, a2, a3 = thirds(away_a, across(away_a))
    moving_a = step(a3, None, 3)
    home_b, away_b = expert(2 * d0, down_b, down_bx, moving_a, down_c)
    down_cx = relay(down_c)
    moving_a = step(after(a2, down_bx, down_c), moving_a, 2)
    b1, b2, b3 = thirds(away_b, across(after(away_b, moving_a, down_cx)))
    moving_a = step(a1, moving_a, 1)
    moving_b = step(b3, None, 3)
    home_c, away_c = expert(2 * (d0 + d1), down_c, down_cx, b3)
    c1, c2, c3 = thirds(away_c, across(after(away_c, moving_a)))
    moving_b = step(b2, moving_b, 2)
    moving_c = step(c3, None, 3)
    moving_b = step(b1, moving_b, 1)
    moving_c = step(c2, moving_c, 2)
    moving_c = step(c1, moving_c, 1)
    results = [finish(home_a, moving_a), finish(home_b, moving_b), finish(home_c, moving_c)]
    return jnp.concatenate(results, axis=1)


def on_device(tokens, expert_ids, combine_weights, gate_weight, up_weight, down_weight):
    line = (
        lax.axis_size("parts") == 2
        and lax.axis_size("node") == 2
        and lax.axis_size("local") == 8
        and tokens.shape == (128, 3584)
        and gate_weight.shape[2] == 512
    )
    form = line_exchange if line else packed_exchange
    return form(tokens, expert_ids, combine_weights, gate_weight, up_weight, down_weight)


def solution(mesh):
    in_specs = (
        P(("parts", "node", "local"), None),
        P(("parts", "node", "local"), None),
        P(("parts", "node", "local"), None),
        P(("node", "local"), None, None),
        P(("node", "local"), None, None),
        P(("node", "local"), None, None),
    )
    out_specs = P(("parts", "node", "local"), None)
    return jax.shard_map(
        on_device, mesh=mesh, in_specs=in_specs, out_specs=out_specs, check_vma=False
    )
```

```python
import functools

import jax
import jax.numpy as jnp
from jax import lax
from jax.experimental import pallas as pl
from jax.experimental.pallas import tpu as pltpu
from jax.sharding import PartitionSpec as P

TILE = 256
LANES = 128
STEPS = 4
GATE_ROWS = (512, 768, 512)
UP_ROWS = (512, 1024, 256)
DOWN_COLUMNS = (1024, 1280, 1280)


def slot_tables(routes, first_expert, expert_count, capacity, expert_total):
    options = jnp.arange(expert_total, dtype=jnp.int32)
    matches = routes[:, :, None] == options[None, None, :]
    counts = jnp.sum(matches.astype(jnp.int32), axis=1)
    before = jnp.cumsum(counts, axis=0) - counts
    rank_in = jnp.sum(jnp.where(matches, before[:, None, :], 0), axis=2)
    local_index = routes - first_expert
    inside = (local_index >= 0) & (local_index < expert_count)
    return (local_index * capacity + rank_in, inside)


def dispatch_matrix(slot_index, inside, total_slots):
    positions = jnp.arange(total_slots, dtype=jnp.int32)
    matches = (slot_index[None, :, :] == positions[:, None, None]) & inside[None, :, :]
    return jnp.sum(matches.astype(jnp.float32), axis=2).astype(jnp.bfloat16)


def weight_matrix(slot_index, inside, weights, total_slots):
    positions = jnp.arange(total_slots, dtype=jnp.int32)
    matches = (slot_index[:, :, None] == positions[None, None, :]) & inside[:, :, None]
    spread = jnp.where(matches, weights.astype(jnp.float32)[:, :, None], 0.0)
    return jnp.sum(spread, axis=1).astype(jnp.bfloat16)


def apply_expert(rows, gate_local, up_local, down_local):
    gate_value = jnp.dot(rows, gate_local, preferred_element_type=jnp.float32)
    up_value = jnp.dot(rows, up_local, preferred_element_type=jnp.float32)
    hidden = (jax.nn.silu(gate_value) * up_value).astype(jnp.bfloat16)
    return jnp.dot(hidden, down_local, preferred_element_type=jnp.float32).astype(jnp.bfloat16)


def packed_exchange(tokens, expert_ids, combine_weights, gate_weight, up_weight, down_weight):
    node_count = lax.axis_size("node")
    local_count = lax.axis_size("local")
    per_node = local_count // 2
    expert_total = node_count * per_node
    token_count = tokens.shape[0]
    model_width = tokens.shape[1]
    top_count = expert_ids.shape[1]
    capacity = token_count * top_count * 5 // (4 * expert_total)
    gate_local = gate_weight[0]
    up_local = up_weight[0]
    down_local = down_weight[0]
    rows_all, weights_all = (
        lax.all_gather(tokens, "node", axis=0, tiled=True),
        lax.all_gather(combine_weights, "node", axis=0, tiled=True),
    )
    routes_all = lax.all_gather(expert_ids, "node", axis=0, tiled=True)
    first_expert = lax.axis_index("node") * per_node
    total_slots = per_node * capacity
    routes_blocks = routes_all.reshape(node_count, token_count, top_count)
    slot_index, inside = jax.vmap(
        lambda routes: slot_tables(routes, first_expert, per_node, capacity, expert_total)
    )(routes_blocks)
    placing = jax.vmap(lambda slots, marks: dispatch_matrix(slots, marks, total_slots))(
        slot_index, inside
    )
    row_blocks = rows_all.reshape(node_count, token_count, model_width)
    packed = jnp.einsum(
        "bst,btd->bsd", placing, row_blocks, preferred_element_type=jnp.float32
    ).astype(jnp.bfloat16)
    packed = packed.reshape(node_count, per_node, capacity, model_width).transpose(1, 0, 2, 3)
    outgoing = jnp.broadcast_to(packed[:, None], (per_node, 2, node_count, capacity, model_width))
    outgoing = outgoing.reshape(local_count, node_count * capacity, model_width)
    rows = lax.all_to_all(outgoing, "local", split_axis=0, concat_axis=0, tiled=True)
    in_shape = rows.shape
    flat_rows = rows.reshape(-1, model_width)
    returned = lax.all_to_all(
        apply_expert(flat_rows, gate_local, up_local, down_local).reshape(in_shape),
        "local",
        split_axis=0,
        concat_axis=0,
        tiled=True,
    )
    returned = returned.reshape(per_node, 2, node_count, capacity, model_width).astype(jnp.float32)
    results = (returned[:, 0] + returned[:, 1]).astype(jnp.bfloat16)
    by_block = results.transpose(1, 0, 2, 3).reshape(node_count, total_slots, model_width)
    weight_blocks = weights_all.reshape(node_count, token_count, top_count)
    mixing = jax.vmap(
        lambda slots, marks, weights: weight_matrix(slots, marks, weights, total_slots)
    )(slot_index, inside, weight_blocks)
    contrib = jnp.einsum(
        "bts,bsd->btd", mixing, by_block, preferred_element_type=jnp.float32
    ).astype(jnp.bfloat16)
    contrib = lax.optimization_barrier(contrib)
    summed_out = lax.psum_scatter(
        contrib.astype(jnp.float32).astype(jnp.bfloat16), "node", scatter_dimension=0, tiled=True
    ).astype(jnp.float32)
    return summed_out[0].astype(jnp.bfloat16)


def expert_weights(expert_ids, combine_weights, expert_total):
    options = jnp.arange(expert_total, dtype=jnp.int32)
    matches = expert_ids[:, :, None] == options[None, None, :]
    spread = jnp.where(matches, combine_weights.astype(jnp.float32)[:, :, None], 0.0)
    return jnp.sum(spread, axis=1).astype(jnp.bfloat16)


def add_rounded(first, second):
    return (first.astype(jnp.float32) + second.astype(jnp.float32)).astype(jnp.bfloat16)


def after(x, *earlier):
    return lax.optimization_barrier((x, *earlier))[0] if earlier else x


def dot32(a, b):
    return jnp.dot(a, b, preferred_element_type=jnp.float32)


def hidden_kernel(batches, gate_pieces, up_pieces, where_ref, *refs):
    rows_refs = refs[:batches]
    gates = refs[batches : batches + len(gate_pieces)]
    ups = refs[batches + len(gate_pieces) : -1]
    out_ref = refs[-1]
    step = pl.program_id(0)
    steps_each = pl.num_programs(0) // batches

    def product(rows, pieces, weights):
        total = None
        for (offset, kind), w in zip(pieces, weights):
            if kind < 0:
                columns = slice(offset, offset + w.shape[0])
            else:
                columns = pl.ds(pl.multiple_of(where_ref[kind] + offset, LANES), w.shape[0])
            value = dot32(rows[:, columns], w[...])
            total = value if total is None else total + value
        return total

    def work(rows):
        gate_value = product(rows, gate_pieces, gates)
        up_value = product(rows, up_pieces, ups)
        out_ref[...] = (gate_value / (1.0 + jnp.exp(-gate_value)) * up_value).astype(jnp.bfloat16)

    for b in range(batches):
        pl.when(step // steps_each == b)(functools.partial(work, rows_refs[b]))


def hidden_call(where, rows, gate_parts, up_parts):
    gate_pieces, up_pieces = [p[:2] for p in gate_parts], [p[:2] for p in up_parts]
    gates, ups = [p[2] for p in gate_parts], [p[2] for p in up_parts]
    blocks = [(p[3], p[4]) if len(p) > 3 else (0, p[2].shape[0]) for p in gate_parts + up_parts]
    batches = len(rows)
    steps_each = rows[0].shape[0] // TILE
    width = rows[0].shape[1]
    units = gates[0].shape[1]

    def rows_map(b):
        return lambda i, w: (jnp.clip(i - b * steps_each, 0, steps_each - 1), 0)

    total = batches * steps_each * TILE
    depth = width - LANES
    once = pl.Buffered(1)

    def block_map(block):
        return lambda i, w: (block, 0)

    return pl.pallas_call(
        functools.partial(hidden_kernel, batches, gate_pieces, up_pieces),
        grid_spec=pltpu.PrefetchScalarGridSpec(
            num_scalar_prefetch=1,
            grid=(batches * steps_each,),
            in_specs=[pl.BlockSpec((TILE, width), rows_map(b)) for b in range(batches)]
            + [
                pl.BlockSpec((length, units), block_map(block), pipeline_mode=once)
                for block, length in blocks
            ],
            out_specs=pl.BlockSpec((TILE, units), lambda i, w: (i, 0)),
        ),
        out_shape=jax.ShapeDtypeStruct((total, units), jnp.bfloat16),
        compiler_params=pltpu.CompilerParams(vmem_limit_bytes=30 * 2**20),
        cost_estimate=pl.CostEstimate(
            flops=4 * total * depth * units,
            bytes_accessed=2 * (total * width + 2 * depth * units + total * units),
            transcendentals=total * units,
        ),
    )(where, *rows, *gates, *ups)


def down_kernel(batches, first, width, where_ref, *refs):
    spread_refs = refs[:batches]
    own_refs = refs[batches : 2 * batches]
    other_ref, down_ref, near_ref, far_ref, home_ref, away_ref = refs[2 * batches :]
    step = pl.program_id(0)
    half = width // 2

    def work(spread, own, out_ref):
        chosen = lax.broadcasted_iota(jnp.int32, spread.shape, 1) == where_ref[2]
        scale = jnp.sum(jnp.where(chosen, spread[...].astype(jnp.float32), 0.0), axis=1, keepdims=True)
        for piece, slot in ((near_ref, where_ref[3]), (far_ref, 1 - where_ref[3])):
            source = pl.ds(pl.multiple_of(first + slot * half, LANES), half)
            target = pl.ds(pl.multiple_of(slot * half, LANES), half)
            value = dot32(own[...], down_ref[:, source]) + dot32(other_ref[...], piece[...])
            out_ref[:, target] = (value * scale).astype(jnp.bfloat16)

    for i in range(STEPS):
        b = i * batches // STEPS
        pl.when(step == i)(
            functools.partial(work, spread_refs[b], own_refs[b], home_ref if i == 0 else away_ref)
        )


def down_call(where, rows, own, other, down_local, near, far, first):
    batches = len(rows)
    steps_each = rows[0].shape[0] // TILE
    units = down_local.shape[0]
    width = 2 * near.shape[1]
    last = rows[0].shape[1] // LANES - 1

    def tile_map(b, column):
        return lambda i, w: (jnp.clip(i - b * steps_each, 0, steps_each - 1), column)

    once = pl.Buffered(1)
    total = batches * steps_each * TILE
    return pl.pallas_call(
        functools.partial(down_kernel, batches, first, width),
        grid_spec=pltpu.PrefetchScalarGridSpec(
            num_scalar_prefetch=1,
            grid=(batches * steps_each,),
            in_specs=[pl.BlockSpec((TILE, LANES), tile_map(b, last)) for b in range(batches)]
            + [pl.BlockSpec((TILE, units), tile_map(b, 0)) for b in range(batches)]
            + [pl.BlockSpec((TILE, units), lambda i, w: (i, 0))]
            + [
                pl.BlockSpec(a.shape, lambda i, w: (0, 0), pipeline_mode=once)
                for a in (down_local, near, far)
            ],
            out_specs=[
                pl.BlockSpec((TILE, width), lambda i, w: (0, 0)),
                pl.BlockSpec((TILE, width), lambda i, w: (jnp.maximum(i - 1, 0), 0)),
            ],
        ),
        out_shape=[
            jax.ShapeDtypeStruct((TILE, width), jnp.bfloat16),
            jax.ShapeDtypeStruct((total - TILE, width), jnp.bfloat16),
        ],
        compiler_params=pltpu.CompilerParams(vmem_limit_bytes=30 * 2**20),
        cost_estimate=pl.CostEstimate(
            flops=4 * total * units * width,
            bytes_accessed=2 * (2 * total * units + 2 * units * width + total * width),
            transcendentals=0,
        ),
    )(where, *rows, *own, other, down_local, near, far)


def line_exchange(tokens, expert_ids, combine_weights, gate_weight, up_weight, down_weight):
    node_count = lax.axis_size("node")
    local_count = lax.axis_size("local")
    planes = local_count // 2
    token_count, model_width = tokens.shape
    expert_total = node_count * planes
    gate_local, up_local, down_local = gate_weight[0], up_weight[0], down_weight[0]
    part = lax.axis_index("parts")
    node = lax.axis_index("node")
    plane = lax.axis_index("local") // 2
    side = plane // 2
    match = side == node
    end = (plane == 0) | (plane == planes - 1)
    both = ("node", "local")
    swap_half = [(i, i ^ 1) for i in range(local_count)]
    swap_two = [(0, 1), (1, 0)]

    def line_pairs(step):
        pairs = []
        for h in range(2):
            pairs += [(2 * (p + 1) + h, 2 * p + h) for p in range(planes - step)]
            pairs += [
                (local_count + 2 * (p - 1) + h, local_count + 2 * p + h) for p in range(step, planes)
            ]
        return pairs

    def back_pairs(step):
        return [(b, a) for a, b in line_pairs(step)]

    def across(x):
        return lax.ppermute(x, "node", swap_two)

    half_depth = model_width // 2
    where = jnp.stack([part * half_depth, (1 - part) * half_depth, node * planes + plane, part])
    where = where.astype(jnp.int32)

    def cut(array, offset, length, dim=0):
        begin = part * (half_depth if dim == 0 else length) + offset
        return lax.dynamic_slice_in_dim(array, begin, length, dim)

    def swap(x):
        return lax.ppermute(x, "local", swap_half)

    def relay(x):
        return lax.ppermute(x, "parts", swap_two)

    def line(x, step):
        return lax.ppermute(x, both, line_pairs(step))

    together = lax.optimization_barrier
    g0, g1, g2 = GATE_ROWS
    u0, u1, u2 = UP_ROWS
    d0, d1, d2 = (w // 2 for w in DOWN_COLUMNS)

    table = expert_weights(expert_ids, combine_weights, expert_total)
    table = jnp.pad(table, ((0, 0), (0, LANES - expert_total)))
    mine = jnp.concatenate([tokens, table], axis=1)

    gate_a = swap(cut(gate_local, 0, g0))
    theirs = across(mine)
    pair = jnp.concatenate(
        [jnp.where(node == 0, mine, theirs), jnp.where(node == 0, theirs, mine)], axis=0
    )
    pair, piece = together((pair, cut(gate_local, g0, g1)))
    got1, gate_b, gate_ax = line(pair, 1), swap(piece), relay(gate_a)
    piece = jnp.concatenate([cut(gate_local, g0 + g1, g2), cut(up_local, 0, u0)], axis=0)
    got1, gate_b, gate_ax, piece = together((got1, gate_b, gate_ax, piece))
    got2, both_c, gate_bx = line(got1, 2), swap(piece), relay(gate_b)
    other1 = across(got1)
    pieces = cut(up_local, u0, u1), cut(down_local, 0, d0, 1)
    got2, both_c, gate_bx, other1, pieces = together((got2, both_c, gate_bx, other1, pieces))
    got3, up_b, both_cx = line(got2, 3), swap(pieces[0]), relay(both_c)
    other2 = across(got2)
    slot1 = jnp.where(match, got1, other1)
    early = jnp.concatenate([pair, slot1], axis=0)
    own = [(0, -1, gate_local)], [(0, -1, up_local)]
    own_early = hidden_call(where, [early], *own)
    rest = u0 + u1
    piece = jnp.concatenate([up_local[rest:half_depth], up_local[half_depth + rest :]], axis=0)
    pieces = piece, pieces[1], cut(down_local, 2 * d0, d1, 1), cut(down_local, 2 * (d0 + d1), d2, 1)
    got3, up_b, both_cx, other2, own_early, pieces = together(
        (got3, up_b, both_cx, other2, own_early, pieces)
    )
    up_bx, up_c, down_a = relay(up_b), swap(pieces[0]), swap(pieces[1])
    other3 = across(got3)
    slot2 = jnp.where(match, got2, other2)
    slot3 = jnp.where(
        end,
        jnp.where(match, got3, other3),
        jnp.where(match, after(other1, got3), after(got1, got3)),
    )
    late = jnp.concatenate([slot2, slot3], axis=0)
    own_late = hidden_call(where, [late], *own)
    up_bx, up_c, down_a, own_late, pieces = together((up_bx, up_c, down_a, own_late, pieces))
    down_ax, down_b = relay(down_a), swap(pieces[2])
    crossed = hidden_call(
        where, [early, late],
        [
            (0, 0, gate_a), (g0, 0, gate_b), (g0 + g1, 0, both_c, 0, g2),
            (0, 1, gate_ax), (g0, 1, gate_bx), (g0 + g1, 1, both_cx, 0, g2),
        ],
        [
            (0, 0, both_c, g2 // u0, u0), (u0, 0, up_b),
            (0, 1, both_cx, g2 // u0, u0), (u0, 1, up_bx),
            (rest, -1, up_c, 0, u2), (half_depth + rest, -1, up_c, 1, u2),
        ],
    )
    down_ax, crossed, piece = together((down_ax, crossed, pieces[3]))

    def expert(first, near, far, *earlier):
        return down_call(
            after(where, *earlier), [early, late], [own_early, own_late], crossed,
            down_local, near, far, first,
        )

    def step(rows, moving, k):
        rows = rows if moving is None else add_rounded(rows, moving)
        return lax.ppermute(rows, both, back_pairs(k))

    def thirds(away, arrived):
        away = add_rounded(away, arrived)
        s1, s2, s3 = (away[i * TILE : (i + 1) * TILE] for i in range(3))
        return jnp.where(match, s1, s3), s2, s3

    def finish(home, moving):
        kept = moving.astype(jnp.float32) + home.astype(jnp.float32)
        low, high = kept[:token_count], kept[token_count:]
        sent = across(jnp.where(node == 0, high, low).astype(jnp.bfloat16))
        return (jnp.where(node == 0, low, high) + sent.astype(jnp.float32)).astype(jnp.bfloat16)

    down_bx, down_c = relay(down_b), swap(piece)
    home_a, away_a = expert(0, down_a, down_ax)
    a1, a2, a3 = thirds(away_a, across(after(away_a, down_b)))
    moving_a = step(a3, None, 3)
    home_b, away_b = expert(2 * d0, down_b, down_bx, moving_a, down_c)
    down_cx = relay(down_c)
    moving_a = step(after(a2, down_bx, down_c), moving_a, 2)
    b1, b2, b3 = thirds(away_b, across(after(away_b, moving_a, down_cx)))
    moving_a = step(a1, moving_a, 1)
    moving_b = step(b3, None, 3)
    home_c, away_c = expert(2 * (d0 + d1), down_c, down_cx, b3)
    c1, c2, c3 = thirds(away_c, across(after(away_c, moving_a)))
    moving_b = step(b2, moving_b, 2)
    moving_c = step(c3, None, 3)
    moving_b = step(b1, moving_b, 1)
    moving_c = step(c2, moving_c, 2)
    moving_c = step(c1, moving_c, 1)
    results = [finish(home_a, moving_a), finish(home_b, moving_b), finish(home_c, moving_c)]
    return jnp.concatenate(results, axis=1)


def on_device(tokens, expert_ids, combine_weights, gate_weight, up_weight, down_weight):
    line = (
        lax.axis_size("parts") == 2
        and lax.axis_size("node") == 2
        and lax.axis_size("local") == 8
        and tokens.shape == (128, 3584)
        and gate_weight.shape[2] == 512
    )
    form = line_exchange if line else packed_exchange
    return form(tokens, expert_ids, combine_weights, gate_weight, up_weight, down_weight)


def solution(mesh):
    in_specs = (
        P(("parts", "node", "local"), None),
        P(("parts", "node", "local"), None),
        P(("parts", "node", "local"), None),
        P(("node", "local"), None, None),
        P(("node", "local"), None, None),
        P(("node", "local"), None, None),
    )
    out_specs = P(("parts", "node", "local"), None)
    return jax.shard_map(
        on_device, mesh=mesh, in_specs=in_specs, out_specs=out_specs, check_vma=False
    )
```
